256 devices in a mesh: user: 4 (over x), heads: 2 (over y_lo), ctx: 32 (over y_hi, z, core).
Axes of the slice: x: 4, y: 4 (y_hi: 2, y_lo: 2; y = y_hi * 2 + y_lo), z: 8, core: 2. Of those that a mesh axis runs over, the one named last changes fastest.
Arguments:
- keys: bfloat16 [65536, 512], P(('user', 'ctx'), 'heads'), parts along dimension 0, may hold values from -6 to 6
- values: bfloat16 [65536, 512], P(('user', 'ctx'), 'heads'), parts along dimension 0, may hold values from -6 to 6
- queries: bfloat16 [4, 98304, 128], P('heads', ('user', 'ctx')), parts along dimension 1, may hold values from -240 to 240
- positions: int32 [98304], P(('user', 'ctx')), parts along dimension 0, may hold values from 0 to 16383
Outputs:
- attended: bfloat16 [4, 98304, 128], P('heads', ('user', 'ctx')), parts along dimension 1
The draws below stay inside these ranges and needn't reach their ends.
There are 4 independent parts, one for each index of `user`. The reference program is written for one: setup_inputs(seed, part) draws one part's arguments, and reference() takes and returns one part's arrays. A program takes and returns all parts, laid end to end along the dimension named above; each array names one. Nothing has to cross between parts.
All inputs are finite; a program needn't handle non-finite values.
Results may differ from the reference program's by a relative error of at most 0.008.
The reference program's roundings to bfloat16 on the way count: a program that leaves them out, or rounds other values in their place, can miss the bound.
Values may be sent and summed in bfloat16 or wider, within the bound.
No kernel may reach another device: no remote copies, remote signals or barrier semaphores. Data moves between devices by JAX's collectives and lax.ppermute only.
A program may use at most 128 MiB of HBM per device.

```python
import math
import jax
import jax.numpy as jnp
from jax import lax

WINDOW = 16384
KV_HEADS = 4
HEAD_DIM = 128
QUERY_DEV = 768
QUERIES = 24576


def draw_queries(key, part):
    first_key = jax.random.fold_in(jax.random.fold_in(key, 11), 0)
    base = jax.random.truncated_normal(first_key, -4.0, 4.0, (KV_HEADS, QUERIES, HEAD_DIM), jnp.float32)
    return base.astype(jnp.bfloat16)


def set_ends(drawn, key, low, largest):
    spot = [jax.random.randint(jax.random.fold_in(key, axis), (), 0, length) for axis, length in enumerate(drawn.shape)]
    main_axis = drawn.shape.index(max(drawn.shape))
    next_to = spot[:main_axis] + [(spot[main_axis] + 1) % drawn.shape[main_axis]] + spot[main_axis + 1:]
    return drawn.at[tuple(spot)].set(low).at[tuple(next_to)].set(largest)


def steps_of(own_key, extent, shards, smallest, high):
    loudness = 1.0
    for axis_at, parts in shards:
        heights = jax.random.uniform(jax.random.fold_in(jax.random.fold_in(own_key, 6), axis_at), (parts,), jnp.float32, smallest / len(shards), high / len(shards))
        loudness = loudness * jnp.repeat(jnp.exp(heights), extent[axis_at] // parts).reshape((-1,) + (1,) * (len(extent) - 1 - axis_at))
    return loudness


def normal_values(stream_key, extent, deviation, most, cuts=(), kind=jnp.bfloat16):
    entries = deviation * jax.random.normal(stream_key, extent, jnp.float32)
    if cuts:
        entries = entries * steps_of(stream_key, extent, cuts, -0.22, 0.18)
    return jnp.clip(entries, -most, most).astype(kind)


def setup_inputs(seed: int = 0, part: int = 0) -> dict:
    seeds = jax.random.split(jax.random.key(seed), 5)
    part_keys = jax.random.split(jax.random.fold_in(seeds[4], part), 5)
    keys = normal_values(part_keys[0], (WINDOW, KV_HEADS * HEAD_DIM), 1.0, 6.0, ((0, 32), (1, 2)))
    values = normal_values(part_keys[1], (WINDOW, KV_HEADS * HEAD_DIM), 1.0, 6.0, ((0, 32), (1, 2)))
    queries = draw_queries(jax.random.fold_in(jax.random.fold_in(seeds[4], part), 71), part)
    positions = set_ends(jax.random.randint(part_keys[3], (QUERIES,), 0, WINDOW), jax.random.fold_in(part_keys[3], 1), 0, WINDOW - 1).astype(jnp.int32)
    return {"keys": keys, "values": values, "queries": queries, "positions": positions}


def compress(signal):
    length = signal.shape[0]
    reordered = jnp.concatenate([signal[0::2], signal[1::2][::-1]], axis=0)
    spectrum = jnp.fft.fft(reordered, axis=0)
    index = jnp.arange(length // 2).astype(jnp.float32)[:, None]
    kept = spectrum[:length // 2]
    coeffs = jnp.real(kept) * jnp.cos(math.pi * index / (2 * length)) + jnp.imag(kept) * jnp.sin(math.pi * index / (2 * length))
    weight = jnp.where(index == 0.0, 1.0 / length, 2.0 / length)
    scaled = coeffs * weight
    twisted = lax.complex(scaled * jnp.cos(math.pi * index / length), scaled * jnp.sin(math.pi * index / length))
    padded = jnp.concatenate([twisted, jnp.zeros_like(twisted)], axis=0)
    return jnp.real(jnp.fft.ifft(padded, axis=0))[:length // 2] * length

def inverse_freq(width):
    return jnp.exp(jnp.arange(width // 2).astype(jnp.float32) * (-2.0 * math.log(500000.0) / width))

def rotate_rows(block, places):
    width = block.shape[-1]
    half = width // 2
    angles = places[:, None] * inverse_freq(width)[None, :]
    cosine = jnp.cos(angles)
    sine = jnp.sin(angles)
    first = block[..., :half]
    second = block[..., half:]
    return jnp.concatenate([first * cosine - second * sine, second * cosine + first * sine], axis=-1)

def reference(keys, values, queries, positions):
    key_small = compress(keys.astype(jnp.float32)).astype(jnp.bfloat16)
    value_small = compress(values.astype(jnp.float32)).astype(jnp.bfloat16)
    kept_len = key_small.shape[0]
    places = jnp.arange(kept_len).astype(jnp.float32)
    query_places = positions.astype(jnp.float32)
    scaling = 1.0 / math.sqrt(HEAD_DIM)
    results = []
    for head_index in range(KV_HEADS):
        low = head_index * HEAD_DIM
        key_head = rotate_rows(key_small[:, low:low + HEAD_DIM].astype(jnp.float32), places).astype(jnp.bfloat16)
        value_head = value_small[:, low:low + HEAD_DIM]
        query_head = rotate_rows(queries[head_index].astype(jnp.float32), query_places).astype(jnp.bfloat16)
        blocks = query_head.reshape(QUERIES // QUERY_DEV, QUERY_DEV, HEAD_DIM)

        def attend_block(query_block):
            scores = jnp.dot(query_block, key_head.T, preferred_element_type=jnp.float32) * scaling
            top = lax.optimization_barrier(jnp.max(scores, axis=1, keepdims=True))
            expo = jnp.exp(scores - top)
            denom = lax.optimization_barrier(jnp.sum(expo, axis=1, keepdims=True))
            summed = jnp.dot(expo.astype(jnp.bfloat16), value_head, preferred_element_type=jnp.float32)
            return (summed / denom).astype(jnp.bfloat16)
        results.append(lax.map(attend_block, blocks).reshape(QUERIES, HEAD_DIM))
    return jnp.stack(results)
```

```python
import functools
import math

import jax
import jax.numpy as jnp
import ml_dtypes
import numpy as np
from jax import lax
from jax.experimental import pallas as pl
from jax.experimental.pallas import tpu as pltpu
from jax.sharding import Mesh
from jax.sharding import PartitionSpec as P

WINDOW = 16384
KEPT = WINDOW // 2
HEAD = 128
HALF = HEAD // 2
COLUMNS = 16
BASE = 128
ROWS = 136
THETA = 500000.0
BF16 = jnp.bfloat16
F32 = jnp.float32
SWAP = [(0, 1), (1, 0)]


def split(matrix):
    high = matrix.astype(ml_dtypes.bfloat16)
    low = (matrix - high.astype(np.float64)).astype(ml_dtypes.bfloat16)
    return high, low


@functools.cache
def transform_tables(sources):
    per_source = BASE // sources
    order = np.arange(BASE)
    a = per_source * (order % sources) + order // sources
    b = np.arange(BASE)
    k0 = np.arange(ROWS)
    live = (k0 <= BASE).astype(np.float64)[:, None]
    t0 = np.arange(64)
    t1 = np.arange(128)
    k1 = np.arange(-32, 32)
    angle = 2 * np.pi * (np.outer(k0, a) % 256) / 256
    first = np.concatenate([np.cos(angle) * live, -np.sin(angle) * live])
    first = np.concatenate(split(first), axis=1)
    angle = np.pi * np.outer(k0, 2 * b + 1) / (2 * WINDOW)
    twist = np.stack([np.cos(angle), np.sin(angle)]).astype(np.float32)
    angle_b = np.pi * (np.outer(2 * b + 1, k1) % 256) / 128
    angle_t = np.pi * (np.outer(k1, 2 * t0 + 1) % 128) / 64
    real = np.concatenate([np.cos(angle_b) @ np.cos(angle_t), np.sin(angle_b) @ np.cos(angle_t)])
    imag = np.concatenate([np.cos(angle_b) @ np.sin(angle_t), np.sin(angle_b) @ np.sin(angle_t)])
    zero = np.zeros_like(real)
    middle = np.concatenate(
        [
            np.concatenate([real, zero, imag, zero], axis=1),
            np.concatenate([zero, real, zero, imag], axis=1),
        ]
    )
    middle = np.stack(split(middle))
    weight = np.where((k0 == 0) | (k0 == BASE), 1.0 / WINDOW, 2.0 / WINDOW)[:, None] * live
    angle = np.pi * np.outer(k0, 2 * np.tile(t0, 2) + 1) / WINDOW
    untwist = np.stack([weight * np.cos(angle), weight * np.sin(angle)]).astype(np.float32)
    angle = 2 * np.pi * (np.outer(t1, k0) % 256) / 256
    last = np.concatenate([np.cos(angle) * live.T, -np.sin(angle) * live.T], axis=1)
    last = np.stack(split(last))
    return first, twist, middle, untwist, last


def inverse_freq():
    return jnp.exp(jnp.arange(HALF).astype(F32) * (-2.0 * math.log(THETA) / HEAD))


def pack_kernel(core_ref, keys_ref, values_ref, other_ref, out_ref):
    core = core_ref[0]
    tokens = keys_ref.shape[0]
    heads, parts = 2, out_ref.shape[0] // 2
    mine = jnp.where(core == 0, keys_ref[...].astype(F32), values_ref[...].astype(F32))
    for block, place in ((mine, core), (other_ref[...].astype(F32), 1 - core)):
        turned = block.T
        at = pl.multiple_of(place * tokens, 128)
        for head in range(heads):
            for part in range(parts):
                low = head * HEAD + part * 8
                rows = jnp.concatenate(
                    [turned[low : low + 8], turned[low + HALF : low + HALF + 8]], axis=0
                )
                out_ref[head * parts + part, :, pl.ds(at, tokens)] = rows.astype(BF16)


def halves(block):
    high = block.astype(BF16)
    return high, (block - high.astype(F32)).astype(BF16)


def dot(left, right):
    return jnp.dot(left, right, preferred_element_type=F32)


def transform_kernel(
    x_ref, first_ref, twist_ref, middle_ref, untwist_ref, last_ref, cos_ref, sin_ref, out_ref,
    wide_ref, rows_ref,
):
    sources, columns, run = x_ref.shape
    for source in range(sources):
        block = x_ref[source].astype(F32)
        for i in range(run // BASE):
            at = (i * sources + source) * columns
            wide_ref[pl.ds(at, columns), :] = block[:, i * BASE : i * BASE + BASE]
    pieces = [wide_ref[pl.ds(column, BASE, stride=columns), :] for column in range(columns)]
    x = jnp.concatenate(pieces, axis=1).astype(BF16)
    cosine, sine = twist_ref[0], twist_ref[1]
    z_real, z_imag = [], []
    for pair in range(columns // 2):
        xp = x[:, pair * 256 : pair * 256 + 256]
        one = dot(first_ref[...], jnp.concatenate([xp, xp], axis=0))
        parts = []
        for which in range(2):
            real = one[:ROWS, which * BASE : which * BASE + BASE]
            imag = one[ROWS:, which * BASE : which * BASE + BASE]
            parts.append(real * cosine + imag * sine)
            parts.append(imag * cosine - real * sine)
        high, low = halves(jnp.concatenate(parts, axis=1))
        two = (
            dot(high, middle_ref[0]) + dot(low, middle_ref[0]) + dot(high, middle_ref[1])
        )
        real, imag = two[:, :BASE], two[:, BASE:]
        z_real.append(real * untwist_ref[0] - imag * untwist_ref[1])
        z_imag.append(real * untwist_ref[1] + imag * untwist_ref[0])
    z = jnp.concatenate(
        [jnp.concatenate(z_real, axis=1), jnp.concatenate(z_imag, axis=1)], axis=0
    )
    high, low = halves(z)
    y = dot(last_ref[0], high) + dot(last_ref[0], low) + dot(last_ref[1], high)
    rows_ref[...] = y.T
    steps = rows_ref.shape[0] // columns
    for step in range(steps):
        token = rows_ref[pl.ds(step, columns, stride=steps), :].astype(BF16).astype(F32)
        here = pl.ds(step * BASE, BASE)
        cosine, sine = cos_ref[:, here], sin_ref[:, here]
        up, down = token[:8], token[8:]
        turned = jnp.concatenate(
            [up * cosine - down * sine, down * cosine + up * sine], axis=0
        )
        out_ref[:, here] = turned.astype(BF16)


def attend_kernel(q_ref, kv_ref, order_ref, out_ref, *, block, scale):
    parts, _, columns, tokens = kv_ref.shape
    q = q_ref[...]
    rows = q.shape[0]
    count = tokens // block

    def scores(step):
        keys = kv_ref[:, 0, :, pl.ds(step * block, block)].reshape(parts * columns, block)
        return dot(q, keys)

    best = jnp.full((rows, 1), -jnp.inf, F32)
    total = jnp.zeros((rows, 1), F32)
    accum = jnp.zeros((rows, HEAD), F32)
    upcoming = scores(0)
    for step in range(count):
        current = upcoming
        if step + 1 < count:
            upcoming = scores(step + 1)
        fresh = jnp.maximum(best, jnp.max(current, axis=1, keepdims=True))
        shrink = jnp.exp2((best - fresh) * scale)
        expo = jnp.exp2((current - fresh) * scale)
        total = total * shrink + jnp.sum(expo, axis=1, keepdims=True)
        values = kv_ref[:, 1, :, pl.ds(step * block, block)].reshape(parts * columns, block)
        summed = lax.dot_general(
            expo.astype(BF16), values, (((1,), (1,)), ((), ())), preferred_element_type=F32
        )
        accum = accum * shrink + summed
        best = fresh
    result = (accum / total).astype(BF16)
    out_ref[...] = dot(result, order_ref[...]).astype(BF16)


def attend(q, kv, order):
    rows = q.shape[0]
    row_block = 256
    kernel = functools.partial(
        attend_kernel, block=1024, scale=math.log2(math.e) / math.sqrt(HEAD)
    )
    return pl.pallas_call(
        kernel,
        grid=(rows // row_block,),
        in_specs=[
            pl.BlockSpec((row_block, HEAD), lambda i: (i, 0)),
            pl.BlockSpec(kv.shape, lambda i: (0, 0, 0, 0)),
            pl.BlockSpec(order.shape, lambda i: (0, 0)),
        ],
        out_specs=pl.BlockSpec((row_block, HEAD), lambda i: (i, 0)),
        out_shape=jax.ShapeDtypeStruct(q.shape, BF16),
        compiler_params=pltpu.CompilerParams(vmem_limit_bytes=48 * 1024 * 1024),
        name="attend",
    )(q, kv, order)


def on_device(keys, values, queries, positions):
    core = lax.axis_index("core")
    head = lax.axis_index("yhi")
    place = lax.axis_index("z")
    parts = lax.axis_size("z")
    sources = 2 * parts
    tokens = keys.shape[0]

    other = lax.ppermute(jnp.where(core == 0, values, keys), "core", SWAP)
    vmem = pl.BlockSpec(memory_space=pltpu.VMEM)
    packed = pl.pallas_call(
        pack_kernel,
        in_specs=[pl.BlockSpec(memory_space=pltpu.SMEM), vmem, vmem, vmem],
        out_specs=vmem,
        out_shape=jax.ShapeDtypeStruct((sources, COLUMNS, 2 * tokens), BF16),
        name="pack",
    )(core[None].astype(jnp.int32), keys, values, other)
    received = lax.all_to_all(packed, ("yhi", "z"), 0, 0, tiled=True)

    freq = inverse_freq()
    index = jnp.arange(KEPT)
    places = (64 * (index % BASE) + index // BASE).astype(F32)
    angles = lax.dynamic_slice(freq, (8 * place,), (8,))[:, None] * places[None, :]
    cosine = jnp.where(core == 0, jnp.cos(angles), 1.0)
    sine = jnp.where(core == 0, jnp.sin(angles), 0.0)
    first, twist, middle, untwist, last = map(jnp.asarray, transform_tables(sources))
    small = pl.pallas_call(
        transform_kernel,
        in_specs=[vmem] * 8,
        out_specs=vmem,
        out_shape=jax.ShapeDtypeStruct((COLUMNS, KEPT), BF16),
        scratch_shapes=[
            pltpu.VMEM((BASE * COLUMNS, BASE), F32),
            pltpu.VMEM((64 * COLUMNS, BASE), F32),
        ],
        compiler_params=pltpu.CompilerParams(vmem_limit_bytes=40 * 1024 * 1024),
        name="transform",
    )(received, first, twist, middle, untwist, last, cosine, sine)

    angles = positions.astype(F32)[:, None] * freq[None, :]
    cosine, sine = jnp.cos(angles), jnp.sin(angles)
    wide = queries.astype(F32)
    up, down = wide[..., :HALF], wide[..., HALF:]
    turned = jnp.concatenate(
        [up * cosine - down * sine, down * cosine + up * sine], axis=-1
    ).astype(BF16)
    lane = jnp.arange(HEAD)
    order = (
        lane[:, None] == (((lane % 16) // 8) * HALF + (lane // 16) * 8 + lane % 8)[None, :]
    ).astype(BF16)
    turned = jnp.einsum("hqd,de->hqe", turned, order, preferred_element_type=F32).astype(BF16)
    own = jnp.where(head == 0, turned[0], turned[1])
    guest = lax.ppermute(jnp.where(head == 0, turned[1], turned[0]), "yhi", SWAP)

    gathered = lax.all_gather(small, ("z", "core"), axis=0, tiled=True)
    kv = gathered.reshape(parts, 2, COLUMNS, KEPT)
    back = order.T
    returned = lax.ppermute(attend(guest, kv, back), "yhi", SWAP)
    kept = attend(own, kv, back)
    return jnp.where(
        head == 0, jnp.stack([kept, returned]), jnp.stack([returned, kept])
    )


def solution(mesh):
    shape = mesh.devices.shape
    fine = Mesh(
        mesh.devices.reshape(shape[0], shape[1], 2, shape[2] // 4, 2),
        ("user", "heads", "yhi", "z", "core"),
    )
    tokens = ("user", "yhi", "z", "core")
    return jax.shard_map(
        on_device,
        mesh=fine,
        in_specs=(P(tokens, "heads"), P(tokens, "heads"), P("heads", tokens, None), P(tokens)),
        out_specs=P("heads", tokens, None),
        check_vma=False,
    )
```

```python
import functools
import math

import jax
import jax.numpy as jnp
import ml_dtypes
import numpy as np
from jax import lax
from jax.experimental import pallas as pl
from jax.experimental.pallas import tpu as pltpu
from jax.sharding import Mesh
from jax.sharding import PartitionSpec as P

WINDOW = 16384
KEPT = WINDOW // 2
HEAD = 128
HALF = HEAD // 2
COLUMNS = 16
BASE = 128
ROWS = 136
THETA = 500000.0
BF16 = jnp.bfloat16
F32 = jnp.float32
SWAP = [(0, 1), (1, 0)]


def split(matrix):
    high = matrix.astype(ml_dtypes.bfloat16)
    low = (matrix - high.astype(np.float64)).astype(ml_dtypes.bfloat16)
    return high, low


@functools.cache
def transform_tables(sources):
    per_source = BASE // sources
    order = np.arange(BASE)
    a = per_source * (order % sources) + order // sources
    b = np.arange(BASE)
    k0 = np.arange(ROWS)
    live = (k0 <= BASE).astype(np.float64)[:, None]
    t0 = np.arange(64)
    t1 = np.arange(128)
    k1 = np.arange(-32, 32)
    angle = 2 * np.pi * (np.outer(k0, a) % 256) / 256
    first = np.concatenate([np.cos(angle) * live, -np.sin(angle) * live])
    first = np.concatenate(split(first), axis=1)
    angle = np.pi * np.outer(k0, 2 * b + 1) / (2 * WINDOW)
    twist = np.stack([np.cos(angle), np.sin(angle)]).astype(np.float32)
    angle_b = np.pi * (np.outer(2 * b + 1, k1) % 256) / 128
    angle_t = np.pi * (np.outer(k1, 2 * t0 + 1) % 128) / 64
    real = np.concatenate([np.cos(angle_b) @ np.cos(angle_t), np.sin(angle_b) @ np.cos(angle_t)])
    imag = np.concatenate([np.cos(angle_b) @ np.sin(angle_t), np.sin(angle_b) @ np.sin(angle_t)])
    zero = np.zeros_like(real)
    middle = np.concatenate(
        [
            np.concatenate([real, zero, imag, zero], axis=1),
            np.concatenate([zero, real, zero, imag], axis=1),
        ]
    )
    middle = np.stack(split(middle))
    weight = np.where((k0 == 0) | (k0 == BASE), 1.0 / WINDOW, 2.0 / WINDOW)[:, None] * live
    angle = np.pi * np.outer(k0, 2 * np.tile(t0, 2) + 1) / WINDOW
    untwist = np.stack([weight * np.cos(angle), weight * np.sin(angle)]).astype(np.float32)
    angle = 2 * np.pi * (np.outer(t1, k0) % 256) / 256
    last = np.concatenate([np.cos(angle) * live.T, -np.sin(angle) * live.T], axis=1)
    last = np.stack(split(last))
    return first, twist, middle, untwist, last


def inverse_freq():
    return jnp.exp(jnp.arange(HALF).astype(F32) * (-2.0 * math.log(THETA) / HEAD))


def choose_kernel(core_ref, keys_ref, values_ref, mine_ref, send_ref, sems):
    def move(mine, send):
        first = pltpu.make_async_copy(send, send_ref, sems.at[0])
        second = pltpu.make_async_copy(mine, mine_ref, sems.at[1])
        first.start()
        second.start()
        first.wait()
        second.wait()

    pl.when(core_ref[0] == 0)(lambda: move(keys_ref, values_ref))
    pl.when(core_ref[0] != 0)(lambda: move(values_ref, keys_ref))


def pack_kernel(core_ref, mine_ref, other_ref, out_ref):
    core = core_ref[0]
    tokens = mine_ref.shape[0]
    heads, parts = 2, out_ref.shape[0] // 2
    for block_ref, place in ((mine_ref, core), (other_ref, 1 - core)):
        turned = block_ref[...].astype(F32).T
        at = pl.multiple_of(place * tokens, 128)
        for head in range(heads):
            for part in range(parts):
                low = head * HEAD + part * 8
                rows = jnp.concatenate(
                    [turned[low : low + 8], turned[low + HALF : low + HALF + 8]], axis=0
                )
                out_ref[head * parts + part, :, pl.ds(at, tokens)] = rows.astype(BF16)


def halves(block):
    high = block.astype(BF16)
    return high, (block - high.astype(F32)).astype(BF16)


def dot(left, right):
    return jnp.dot(left, right, preferred_element_type=F32)


def transform_kernel(
    x_ref, cos_ref, sin_ref, first_hbm, twist_hbm, middle_hbm, untwist_hbm, last_hbm, *refs
):
    *out_refs, first_ref, twist_ref, middle_ref, untwist_ref, last_ref, wide_ref, rows_ref, sems = refs
    copies = [
        pltpu.make_async_copy(source, target, sems.at[i])
        for i, (source, target) in enumerate(
            (
                (first_hbm, first_ref),
                (twist_hbm, twist_ref),
                (middle_hbm, middle_ref),
                (untwist_hbm, untwist_ref),
                (last_hbm, last_ref),
            )
        )
    ]
    for copy in copies:
        copy.start()
    sources, columns, run = x_ref.shape
    for source in range(sources):
        block = x_ref[source].astype(F32)
        for i in range(run // BASE):
            at = (i * sources + source) * columns
            wide_ref[pl.ds(at, columns), :] = block[:, i * BASE : i * BASE + BASE]
    pieces = [wide_ref[pl.ds(column, BASE, stride=columns), :] for column in range(columns)]
    x = jnp.concatenate(pieces, axis=1).astype(BF16)
    for copy in copies:
        copy.wait()
    cosine, sine = twist_ref[0], twist_ref[1]
    z_real, z_imag = [], []
    for pair in range(columns // 2):
        xp = x[:, pair * 256 : pair * 256 + 256]
        one = dot(first_ref[...], jnp.concatenate([xp, xp], axis=0))
        parts = []
        for which in range(2):
            real = one[:ROWS, which * BASE : which * BASE + BASE]
            imag = one[ROWS:, which * BASE : which * BASE + BASE]
            parts.append(real * cosine + imag * sine)
            parts.append(imag * cosine - real * sine)
        high, low = halves(jnp.concatenate(parts, axis=1))
        two = (
            dot(high, middle_ref[0]) + dot(low, middle_ref[0]) + dot(high, middle_ref[1])
        )
        real, imag = two[:, :BASE], two[:, BASE:]
        z_real.append(real * untwist_ref[0] - imag * untwist_ref[1])
        z_imag.append(real * untwist_ref[1] + imag * untwist_ref[0])
    z = jnp.concatenate(
        [jnp.concatenate(z_real, axis=1), jnp.concatenate(z_imag, axis=1)], axis=0
    )
    high, low = halves(z)
    y = dot(last_ref[0], high) + dot(last_ref[0], low) + dot(last_ref[1], high)
    rows_ref[...] = y.T
    steps = rows_ref.shape[0] // columns
    for step in range(steps):
        token = rows_ref[pl.ds(step, columns, stride=steps), :].astype(BF16).astype(F32)
        here = pl.ds(step * BASE, BASE)
        cosine, sine = cos_ref[:, here], sin_ref[:, here]
        up, down = token[:8], token[8:]
        turned = jnp.concatenate(
            [up * cosine - down * sine, down * cosine + up * sine], axis=0
        )
        chunk, place = divmod(step * BASE, out_refs[0].shape[1])
        out_refs[chunk][:, pl.ds(place, BASE)] = turned.astype(BF16)


def attend_rows(q, kv_ref, core, order, *, block, scale):
    _, width, tokens = kv_ref.shape
    rows = q.shape[0]
    count = tokens // block

    def scores(step):
        return dot(q, kv_ref[core, :, pl.ds(step * block, block)])

    best = jnp.full((rows, 1), -jnp.inf, F32)
    accum = jnp.zeros((rows, 2 * HEAD), F32)
    ones = jnp.ones((HEAD, block), BF16)
    upcoming = scores(0)
    for step in range(count):
        current = upcoming
        if step + 1 < count:
            upcoming = scores(step + 1)
        fresh = jnp.maximum(best, jnp.max(current, axis=1, keepdims=True))
        shrink = jnp.exp2((best - fresh) * scale)
        expo = jnp.exp2((current - fresh) * scale).astype(BF16)
        values = kv_ref[1 - core, :, pl.ds(step * block, block)]
        summed = lax.dot_general(
            expo,
            jnp.concatenate([values, ones], axis=0),
            (((1,), (1,)), ((), ())),
            preferred_element_type=F32,
        )
        accum = accum * shrink + summed
        best = fresh
    result = (accum[:, :HEAD] / accum[:, HEAD:]).astype(BF16)
    return dot(result, order).astype(BF16)


SCALE = math.log2(math.e) / math.sqrt(HEAD)
ROW_BLOCK = 384
TOKEN_BLOCK = 2048
CHUNKS = 1


def gather_attend_kernel(core_ref, q_ref, order_ref, *refs):
    *blocks, out_ref, kv_ref, sems = refs
    half = len(blocks) // 2
    columns, run = blocks[0].shape

    @pl.when(pl.program_id(0) == 0)
    def _():
        copies = []
        for i, block in enumerate(blocks):
            which, at = divmod(i, half)
            row, chunk = divmod(at, CHUNKS)
            target = kv_ref.at[which, pl.ds(row * columns, columns), pl.ds(chunk * run, run)]
            copies.append(pltpu.make_async_copy(block, target, sems.at[i]))
        for copy in copies:
            copy.start()
        for copy in copies:
            copy.wait()

    out_ref[...] = attend_rows(
        q_ref[...], kv_ref, core_ref[0], order_ref[...], block=TOKEN_BLOCK, scale=SCALE
    )


def attend_kernel(core_ref, q_ref, order_ref, kv_ref, out_ref):
    out_ref[...] = attend_rows(
        q_ref[...], kv_ref, core_ref[0], order_ref[...], block=TOKEN_BLOCK, scale=SCALE
    )


def gather_attend(core, q, order, blocks):
    rows = q.shape[0]
    columns, run = blocks[0].shape
    kv_shape = (2, len(blocks) // (2 * CHUNKS) * columns, CHUNKS * run)
    return pl.pallas_call(
        gather_attend_kernel,
        grid=(rows // ROW_BLOCK,),
        in_specs=[
            pl.BlockSpec(memory_space=pltpu.SMEM),
            pl.BlockSpec((ROW_BLOCK, HEAD), lambda i: (i, 0)),
            pl.BlockSpec(order.shape, lambda i: (0, 0)),
        ]
        + [pl.BlockSpec(memory_space=pl.ANY)] * len(blocks),
        out_specs=[
            pl.BlockSpec((ROW_BLOCK, HEAD), lambda i: (i, 0)),
            pl.BlockSpec(memory_space=pltpu.VMEM),
        ],
        out_shape=[
            jax.ShapeDtypeStruct(q.shape, BF16),
            jax.ShapeDtypeStruct(kv_shape, BF16),
        ],
        scratch_shapes=[pltpu.SemaphoreType.DMA((len(blocks),))],
        compiler_params=pltpu.CompilerParams(vmem_limit_bytes=32 * 1024 * 1024),
        name="gather_attend",
    )(core, q, order, *blocks)


def attend(core, q, order, kv):
    return pl.pallas_call(
        attend_kernel,
        grid=(q.shape[0] // ROW_BLOCK,),
        in_specs=[
            pl.BlockSpec(memory_space=pltpu.SMEM),
            pl.BlockSpec((ROW_BLOCK, HEAD), lambda i: (i, 0)),
            pl.BlockSpec(order.shape, lambda i: (0, 0)),
            pl.BlockSpec(memory_space=pltpu.VMEM),
        ],
        out_specs=pl.BlockSpec((ROW_BLOCK, HEAD), lambda i: (i, 0)),
        out_shape=jax.ShapeDtypeStruct(q.shape, BF16),
        compiler_params=pltpu.CompilerParams(vmem_limit_bytes=32 * 1024 * 1024),
        name="attend",
    )(core, q, order, kv)


def ring_gather(small, parts):
    onward = [(2 * i, 2 * ((i + 1) % parts)) for i in range(parts)]
    onward += [(2 * i + 1, 2 * ((i - 1) % parts) + 1) for i in range(parts)]

    def along(block):
        return lax.ppermute(block, ("z", "core"), onward)

    def across(block):
        return lax.ppermute(block, "core", SWAP)

    a = [along(block) for block in small]
    other = [across(block) for block in small]
    b = [along(block) for block in other]
    mine, theirs = list(small), list(other)
    for step in range(1, parts // 2):
        a_next = [along(block) for block in a]
        a_swapped = [across(block) for block in a]
        b_next = [along(block) for block in b] if step + 1 < parts // 2 else None
        b_swapped = [across(block) for block in b]
        mine += a + b_swapped
        theirs += b + a_swapped
        a, b = a_next, b_next
    return mine + a, theirs + [across(block) for block in a]


def on_device(keys, values, queries, positions):
    core = lax.axis_index("core")
    head = lax.axis_index("yhi")
    place = lax.axis_index("z")
    parts = lax.axis_size("z")
    sources = 2 * parts
    tokens = keys.shape[0]
    core_here = core[None].astype(jnp.int32)

    vmem = pl.BlockSpec(memory_space=pltpu.VMEM)
    smem = pl.BlockSpec(memory_space=pltpu.SMEM)
    hbm = pl.BlockSpec(memory_space=pltpu.HBM)
    chosen = jax.ShapeDtypeStruct(keys.shape, BF16)
    kept_tokens, send = pl.pallas_call(
        choose_kernel,
        in_specs=[smem, hbm, hbm],
        out_specs=[vmem, vmem],
        out_shape=[chosen, chosen],
        scratch_shapes=[pltpu.SemaphoreType.DMA((2,))],
        compiler_params=pltpu.CompilerParams(vmem_limit_bytes=16 * 1024 * 1024),
        name="choose",
    )(core_here, keys, values)
    other = lax.ppermute(send, "core", SWAP)
    packed = pl.pallas_call(
        pack_kernel,
        in_specs=[smem, vmem, vmem],
        out_specs=vmem,
        out_shape=jax.ShapeDtypeStruct((sources, COLUMNS, 2 * tokens), BF16),
        compiler_params=pltpu.CompilerParams(vmem_limit_bytes=16 * 1024 * 1024),
        name="pack",
    )(core_here, kept_tokens, other)
    packed, queries, positions = lax.optimization_barrier((packed, queries, positions))
    received = lax.all_to_all(packed, ("yhi", "z"), 0, 0, tiled=True)

    freq = inverse_freq()
    angles = positions.astype(F32)[:, None] * freq[None, :]
    cosine, sine = jnp.cos(angles), jnp.sin(angles)
    wide = queries.astype(F32)
    up, down = wide[..., :HALF], wide[..., HALF:]
    turned = jnp.concatenate(
        [up * cosine - down * sine, down * cosine + up * sine], axis=-1
    ).astype(BF16)
    lane = jnp.arange(HEAD)
    at = lane // COLUMNS
    away = jnp.where(at % 2 == 1, -1, 1) * ((at + 1) // 2) * jnp.where(core == 0, 1, -1)
    owner = (place + away) % parts
    column = ((lane % COLUMNS) // 8) * HALF + owner * 8 + lane % 8
    order = (lane[:, None] == column[None, :]).astype(BF16)
    turned = jnp.einsum("hqd,de->hqe", turned, order, preferred_element_type=F32).astype(BF16)
    own = jnp.where(head == 0, turned[0], turned[1])
    guest = lax.ppermute(jnp.where(head == 0, turned[1], turned[0]), "yhi", SWAP)

    index = jnp.arange(KEPT)
    places = (64 * (index % BASE) + index // BASE).astype(F32)
    angles = lax.dynamic_slice(freq, (8 * place,), (8,))[:, None] * places[None, :]
    cosine = jnp.where(core == 0, jnp.cos(angles), 1.0)
    sine = jnp.where(core == 0, jnp.sin(angles), 0.0)
    received, own, guest, cosine, sine = lax.optimization_barrier(
        (received, own, guest, cosine, sine)
    )
    tables = transform_tables(sources)
    small = pl.pallas_call(
        transform_kernel,
        in_specs=[vmem] * 3 + [hbm] * 5,
        out_specs=[vmem] * CHUNKS,
        out_shape=[jax.ShapeDtypeStruct((COLUMNS, KEPT // CHUNKS), BF16)] * CHUNKS,
        scratch_shapes=[pltpu.VMEM(t.shape, t.dtype) for t in tables]
        + [
            pltpu.VMEM((BASE * COLUMNS, BASE), F32),
            pltpu.VMEM((64 * COLUMNS, BASE), F32),
            pltpu.SemaphoreType.DMA((len(tables),)),
        ],
        compiler_params=pltpu.CompilerParams(vmem_limit_bytes=32 * 1024 * 1024),
        name="transform",
    )(received, cosine, sine, *map(jnp.asarray, tables))

    mine, theirs = ring_gather(small, parts)
    back = order.T
    first, kv = gather_attend(core_here, guest, back, mine + theirs)
    returned = lax.ppermute(first, "yhi", SWAP)
    kept = attend(core_here, own, back, kv)
    return jnp.where(
        head == 0, jnp.stack([kept, returned]), jnp.stack([returned, kept])
    )


def solution(mesh):
    shape = mesh.devices.shape
    fine = Mesh(
        mesh.devices.reshape(shape[0], shape[1], 2, shape[2] // 4, 2),
        ("user", "heads", "yhi", "z", "core"),
    )
    tokens = ("user", "yhi", "z", "core")
    return jax.shard_map(
        on_device,
        mesh=fine,
        in_specs=(P(tokens, "heads"), P(tokens, "heads"), P("heads", tokens, None), P(tokens)),
        out_specs=P("heads", tokens, None),
        check_vma=False,
    )
```

```python
import functools
import math

import jax
import jax.numpy as jnp
import ml_dtypes
import numpy as np
from jax import lax
from jax.experimental import pallas as pl
from jax.experimental.pallas import tpu as pltpu
from jax.sharding import Mesh
from jax.sharding import PartitionSpec as P

WINDOW = 16384
KEPT = WINDOW // 2
HEAD = 128
HALF = HEAD // 2
COLUMNS = 16
BASE = 128
ROWS = 136
THETA = 500000.0
BF16 = jnp.bfloat16
F32 = jnp.float32
SWAP = [(0, 1), (1, 0)]


def split(matrix):
    high = matrix.astype(ml_dtypes.bfloat16)
    low = (matrix - high.astype(np.float64)).astype(ml_dtypes.bfloat16)
    return high, low


@functools.cache
def transform_tables(sources):
    per_source = BASE // sources
    order = np.arange(BASE)
    a = per_source * (order % sources) + order // sources
    b = np.arange(BASE)
    k0 = np.arange(ROWS)
    live = (k0 <= BASE).astype(np.float64)[:, None]
    t0 = np.arange(64)
    t1 = np.arange(128)
    k1 = np.arange(-32, 32)
    angle = 2 * np.pi * (np.outer(k0, a) % 256) / 256
    first = np.concatenate([np.cos(angle) * live, -np.sin(angle) * live])
    first = np.concatenate(split(first), axis=1)
    angle = np.pi * np.outer(k0, 2 * b + 1) / (2 * WINDOW)
    twist = np.stack([np.cos(angle), np.sin(angle)]).astype(np.float32)
    angle_b = np.pi * (np.outer(2 * b + 1, k1) % 256) / 128
    angle_t = np.pi * (np.outer(k1, 2 * t0 + 1) % 128) / 64
    real = np.concatenate([np.cos(angle_b) @ np.cos(angle_t), np.sin(angle_b) @ np.cos(angle_t)])
    imag = np.concatenate([np.cos(angle_b) @ np.sin(angle_t), np.sin(angle_b) @ np.sin(angle_t)])
    zero = np.zeros_like(real)
    middle = np.concatenate(
        [
            np.concatenate([real, zero, imag, zero], axis=1),
            np.concatenate([zero, real, zero, imag], axis=1),
        ]
    )
    middle = np.stack(split(middle))
    weight = np.where((k0 == 0) | (k0 == BASE), 1.0 / WINDOW, 2.0 / WINDOW)[:, None] * live
    angle = np.pi * np.outer(k0, 2 * np.tile(t0, 2) + 1) / WINDOW
    untwist = np.stack([weight * np.cos(angle), weight * np.sin(angle)]).astype(np.float32)
    angle = 2 * np.pi * (np.outer(t1, k0[:BASE]) % 256) / 256
    last = np.concatenate([np.cos(angle), -np.sin(angle)], axis=1)
    last[:, BASE] = (-1.0) ** t1
    last = np.stack(split(last))
    return first, twist, middle, untwist, last


def inverse_freq():
    return jnp.exp(jnp.arange(HALF).astype(F32) * (-2.0 * math.log(THETA) / HEAD))


def choose_kernel(core_ref, keys_ref, values_ref, mine_ref, send_ref, sems):
    def move(mine, send):
        first = pltpu.make_async_copy(send, send_ref, sems.at[0])
        second = pltpu.make_async_copy(mine, mine_ref, sems.at[1])
        first.start()
        second.start()
        first.wait()
        second.wait()

    pl.when(core_ref[0] == 0)(lambda: move(keys_ref, values_ref))
    pl.when(core_ref[0] != 0)(lambda: move(values_ref, keys_ref))


def pack_kernel(core_ref, mine_ref, other_ref, out_ref):
    core = core_ref[0]
    tokens = mine_ref.shape[0]
    heads, parts = 2, out_ref.shape[0] // 2
    for block_ref, place in ((mine_ref, core), (other_ref, 1 - core)):
        turned = block_ref[...].astype(F32).T
        at = pl.multiple_of(place * tokens, 128)
        for head in range(heads):
            for part in range(parts):
                low = head * HEAD + part * 8
                rows = jnp.concatenate(
                    [turned[low : low + 8], turned[low + HALF : low + HALF + 8]], axis=0
                )
                out_ref[head * parts + part, :, pl.ds(at, tokens)] = rows.astype(BF16)


def halves(block):
    high = block.astype(BF16)
    return high, (block - high.astype(F32)).astype(BF16)


def dot(left, right):
    return jnp.dot(left, right, preferred_element_type=F32)


def transform_kernel(
    x_ref, cos_ref, sin_ref, first_hbm, twist_hbm, middle_hbm, untwist_hbm, last_hbm, *refs
):
    *out_refs, first_ref, twist_ref, middle_ref, untwist_ref, last_ref, wide_ref, rows_ref, sems = refs
    copies = [
        pltpu.make_async_copy(source, target, sems.at[i])
        for i, (source, target) in enumerate(
            (
                (first_hbm, first_ref),
                (twist_hbm, twist_ref),
                (middle_hbm, middle_ref),
                (untwist_hbm, untwist_ref),
                (last_hbm, last_ref),
            )
        )
    ]
    for copy in copies:
        copy.start()
    sources, columns, run = x_ref.shape
    for source in range(sources):
        block = x_ref[source].astype(F32)
        for i in range(run // BASE):
            at = (i * sources + source) * columns
            wide_ref[pl.ds(at, columns), :] = block[:, i * BASE : i * BASE + BASE]
    pieces = [wide_ref[pl.ds(column, BASE, stride=columns), :] for column in range(columns)]
    x = jnp.concatenate(pieces, axis=1).astype(BF16)
    for copy in copies:
        copy.wait()
    cosine, sine = twist_ref[0], twist_ref[1]
    parts = []
    for pair in range(columns // 2):
        xp = x[:, pair * 256 : pair * 256 + 256]
        one = dot(first_ref[...], jnp.concatenate([xp, xp], axis=0))
        part = []
        for which in range(2):
            real = one[:ROWS, which * BASE : which * BASE + BASE]
            imag = one[ROWS:, which * BASE : which * BASE + BASE]
            part.append(real * cosine + imag * sine)
            part.append(imag * cosine - real * sine)
        parts.append(jnp.concatenate(part, axis=1))
    high, low = halves(jnp.concatenate(parts, axis=0))
    two = dot(high, middle_ref[0]) + dot(low, middle_ref[0]) + dot(high, middle_ref[1])
    top = lax.broadcasted_iota(jnp.int32, (BASE, BASE), 0) == 0
    z_real, z_imag = [], []
    for pair in range(columns // 2):
        real = two[pair * ROWS : pair * ROWS + ROWS, :BASE]
        imag = two[pair * ROWS : pair * ROWS + ROWS, BASE:]
        up = real * untwist_ref[0] - imag * untwist_ref[1]
        down = real * untwist_ref[1] + imag * untwist_ref[0]
        z_real.append(up[:BASE])
        z_imag.append(jnp.where(top, up[BASE : BASE + 1], down[:BASE]))
    z = jnp.concatenate(
        [jnp.concatenate(z_real, axis=1), jnp.concatenate(z_imag, axis=1)], axis=0
    )
    high, low = halves(z)
    y = dot(last_ref[0], high) + dot(last_ref[0], low) + dot(last_ref[1], high)
    rows_ref[...] = y.T
    steps = rows_ref.shape[0] // columns
    for step in range(steps):
        token = rows_ref[pl.ds(step, columns, stride=steps), :].astype(BF16).astype(F32)
        here = pl.ds(step * BASE, BASE)
        cosine, sine = cos_ref[:, here], sin_ref[:, here]
        up, down = token[:8], token[8:]
        turned = jnp.concatenate(
            [up * cosine - down * sine, down * cosine + up * sine], axis=0
        )
        chunk, place = divmod(step * BASE, out_refs[0].shape[1])
        out_refs[chunk][:, pl.ds(place, BASE)] = turned.astype(BF16)


def attend_rows(q, kv_ref, core, order, *, block, scale):
    _, width, tokens = kv_ref.shape
    rows = q.shape[0]
    count = tokens // block

    def scores(step):
        return dot(q, kv_ref[core, :, pl.ds(step * block, block)])

    best = jnp.full((rows, 1), -jnp.inf, F32)
    accum = jnp.zeros((rows, 2 * HEAD), F32)
    ones = jnp.ones((HEAD, block), BF16)
    upcoming = scores(0)
    for step in range(count):
        current = upcoming
        if step + 1 < count:
            upcoming = scores(step + 1)
        fresh = jnp.maximum(best, jnp.max(current, axis=1, keepdims=True))
        shrink = jnp.exp2((best - fresh) * scale)
        expo = jnp.exp2((current - fresh) * scale).astype(BF16)
        values = kv_ref[1 - core, :, pl.ds(step * block, block)]
        summed = lax.dot_general(
            expo,
            jnp.concatenate([values, ones], axis=0),
            (((1,), (1,)), ((), ())),
            preferred_element_type=F32,
        )
        accum = accum * shrink + summed
        best = fresh
    result = (accum[:, :HEAD] / accum[:, HEAD:]).astype(BF16)
    return dot(result, order).astype(BF16)


SCALE = math.log2(math.e) / math.sqrt(HEAD)
ROW_BLOCK = 768
TOKEN_BLOCK = 2048
CHUNKS = 1


def gather_attend_kernel(core_ref, q_ref, order_ref, *refs):
    *blocks, out_ref, kv_ref, sems = refs
    half = len(blocks) // 2
    columns, run = blocks[0].shape

    @pl.when(pl.program_id(0) == 0)
    def _():
        copies = []
        for i, block in enumerate(blocks):
            which, at = divmod(i, half)
            row, chunk = divmod(at, CHUNKS)
            target = kv_ref.at[which, pl.ds(row * columns, columns), pl.ds(chunk * run, run)]
            copies.append(pltpu.make_async_copy(block, target, sems.at[i]))
        for copy in copies:
            copy.start()
        for copy in copies:
            copy.wait()

    out_ref[...] = attend_rows(
        q_ref[...], kv_ref, core_ref[0], order_ref[...], block=TOKEN_BLOCK, scale=SCALE
    )


def attend_kernel(core_ref, q_ref, order_ref, kv_ref, out_ref):
    out_ref[...] = attend_rows(
        q_ref[...], kv_ref, core_ref[0], order_ref[...], block=TOKEN_BLOCK, scale=SCALE
    )


def gather_attend(core, q, order, blocks):
    rows = q.shape[0]
    columns, run = blocks[0].shape
    kv_shape = (2, len(blocks) // (2 * CHUNKS) * columns, CHUNKS * run)
    return pl.pallas_call(
        gather_attend_kernel,
        grid=(rows // ROW_BLOCK,),
        in_specs=[
            pl.BlockSpec(memory_space=pltpu.SMEM),
            pl.BlockSpec((ROW_BLOCK, HEAD), lambda i: (i, 0)),
            pl.BlockSpec(order.shape, lambda i: (0, 0)),
        ]
        + [pl.BlockSpec(memory_space=pl.ANY)] * len(blocks),
        out_specs=[
            pl.BlockSpec((ROW_BLOCK, HEAD), lambda i: (i, 0)),
            pl.BlockSpec(memory_space=pltpu.VMEM),
        ],
        out_shape=[
            jax.ShapeDtypeStruct(q.shape, BF16),
            jax.ShapeDtypeStruct(kv_shape, BF16),
        ],
        scratch_shapes=[pltpu.SemaphoreType.DMA((len(blocks),))],
        compiler_params=pltpu.CompilerParams(vmem_limit_bytes=32 * 1024 * 1024),
        name="gather_attend",
    )(core, q, order, *blocks)


def attend(core, q, order, kv):
    return pl.pallas_call(
        attend_kernel,
        grid=(q.shape[0] // ROW_BLOCK,),
        in_specs=[
            pl.BlockSpec(memory_space=pltpu.SMEM),
            pl.BlockSpec((ROW_BLOCK, HEAD), lambda i: (i, 0)),
            pl.BlockSpec(order.shape, lambda i: (0, 0)),
            pl.BlockSpec(memory_space=pltpu.VMEM),
        ],
        out_specs=pl.BlockSpec((ROW_BLOCK, HEAD), lambda i: (i, 0)),
        out_shape=jax.ShapeDtypeStruct(q.shape, BF16),
        compiler_params=pltpu.CompilerParams(vmem_limit_bytes=32 * 1024 * 1024),
        name="attend",
    )(core, q, order, kv)


def ring_gather(small, parts):
    onward = [(2 * i, 2 * ((i + 1) % parts)) for i in range(parts)]
    onward += [(2 * i + 1, 2 * ((i - 1) % parts) + 1) for i in range(parts)]

    def along(block):
        return lax.ppermute(block, ("z", "core"), onward)

    def across(block):
        return lax.ppermute(block, "core", SWAP)

    a = [along(block) for block in small]
    other = [across(block) for block in small]
    b = [along(block) for block in other]
    mine, theirs = list(small), list(other)
    for step in range(1, parts // 2):
        a_next = [along(block) for block in a]
        a_swapped = [across(block) for block in a]
        b_next = [along(block) for block in b] if step + 1 < parts // 2 else None
        b_swapped = [across(block) for block in b]
        mine += a + b_swapped
        theirs += b + a_swapped
        a, b = a_next, b_next
    return mine + a, theirs + [across(block) for block in a]


def on_device(keys, values, queries, positions):
    core = lax.axis_index("core")
    head = lax.axis_index("yhi")
    place = lax.axis_index("z")
    parts = lax.axis_size("z")
    sources = 2 * parts
    tokens = keys.shape[0]
    core_here = core[None].astype(jnp.int32)

    vmem = pl.BlockSpec(memory_space=pltpu.VMEM)
    smem = pl.BlockSpec(memory_space=pltpu.SMEM)
    hbm = pl.BlockSpec(memory_space=pltpu.HBM)
    chosen = jax.ShapeDtypeStruct(keys.shape, BF16)
    kept_tokens, send = pl.pallas_call(
        choose_kernel,
        in_specs=[smem, hbm, hbm],
        out_specs=[vmem, vmem],
        out_shape=[chosen, chosen],
        scratch_shapes=[pltpu.SemaphoreType.DMA((2,))],
        compiler_params=pltpu.CompilerParams(vmem_limit_bytes=16 * 1024 * 1024),
        name="choose",
    )(core_here, keys, values)
    other = lax.ppermute(send, "core", SWAP)
    packed = pl.pallas_call(
        pack_kernel,
        in_specs=[smem, vmem, vmem],
        out_specs=vmem,
        out_shape=jax.ShapeDtypeStruct((sources, COLUMNS, 2 * tokens), BF16),
        compiler_params=pltpu.CompilerParams(vmem_limit_bytes=16 * 1024 * 1024),
        name="pack",
    )(core_here, kept_tokens, other)
    places_here = positions.astype(F32)
    packed, queries, places_here = lax.optimization_barrier((packed, queries, places_here))
    received = lax.all_to_all(packed, ("yhi", "z"), 0, 0, tiled=True)

    freq = inverse_freq()
    angles = places_here[:, None] * freq[None, :]
    cosine, sine = jnp.cos(angles), jnp.sin(angles)
    wide = queries.astype(F32)
    up, down = wide[..., :HALF], wide[..., HALF:]
    turned = jnp.concatenate(
        [up * cosine - down * sine, down * cosine + up * sine], axis=-1
    ).astype(BF16)
    lane = jnp.arange(HEAD)
    at = lane // COLUMNS
    away = jnp.where(at % 2 == 1, -1, 1) * ((at + 1) // 2) * jnp.where(core == 0, 1, -1)
    owner = (place + away) % parts
    column = ((lane % COLUMNS) // 8) * HALF + owner * 8 + lane % 8
    order = (lane[:, None] == column[None, :]).astype(BF16)
    turned = jnp.einsum("hqd,de->hqe", turned, order, preferred_element_type=F32).astype(BF16)
    own = jnp.where(head == 0, turned[0], turned[1])
    guest = lax.ppermute(jnp.where(head == 0, turned[1], turned[0]), "yhi", SWAP)

    index = jnp.arange(KEPT)
    places = (64 * (index % BASE) + index // BASE).astype(F32)
    angles = lax.dynamic_slice(freq, (8 * place,), (8,))[:, None] * places[None, :]
    cosine = jnp.where(core == 0, jnp.cos(angles), 1.0)
    sine = jnp.where(core == 0, jnp.sin(angles), 0.0)
    received, own, guest, cosine, sine = lax.optimization_barrier(
        (received, own, guest, cosine, sine)
    )
    tables = transform_tables(sources)
    small = pl.pallas_call(
        transform_kernel,
        in_specs=[vmem] * 3 + [hbm] * 5,
        out_specs=[vmem] * CHUNKS,
        out_shape=[jax.ShapeDtypeStruct((COLUMNS, KEPT // CHUNKS), BF16)] * CHUNKS,
        scratch_shapes=[pltpu.VMEM(t.shape, t.dtype) for t in tables]
        + [
            pltpu.VMEM((BASE * COLUMNS, BASE), F32),
            pltpu.VMEM((64 * COLUMNS, BASE), F32),
            pltpu.SemaphoreType.DMA((len(tables),)),
        ],
        compiler_params=pltpu.CompilerParams(vmem_limit_bytes=32 * 1024 * 1024),
        name="transform",
    )(received, cosine, sine, *map(jnp.asarray, tables))

    mine, theirs = ring_gather(small, parts)
    back = order.T
    first, kv = gather_attend(core_here, guest, back, mine + theirs)
    returned = lax.ppermute(first, "yhi", SWAP)
    kept = attend(core_here, own, back, kv)
    return jnp.where(
        head == 0, jnp.stack([kept, returned]), jnp.stack([returned, kept])
    )


def solution(mesh):
    shape = mesh.devices.shape
    fine = Mesh(
        mesh.devices.reshape(shape[0], shape[1], 2, shape[2] // 4, 2),
        ("user", "heads", "yhi", "z", "core"),
    )
    tokens = ("user", "yhi", "z", "core")
    return jax.shard_map(
        on_device,
        mesh=fine,
        in_specs=(P(tokens, "heads"), P(tokens, "heads"), P("heads", tokens, None), P(tokens)),
        out_specs=P("heads", tokens, None),
        check_vma=False,
    )
```

```python
import functools
import math

import jax
import jax.numpy as jnp
import ml_dtypes
import numpy as np
from jax import lax
from jax.experimental import pallas as pl
from jax.experimental.pallas import tpu as pltpu
from jax.sharding import Mesh
from jax.sharding import PartitionSpec as P

WINDOW = 16384
KEPT = WINDOW // 2
HEAD = 128
HALF = HEAD // 2
COLUMNS = 16
BASE = 128
ROWS = 136
THETA = 500000.0
BF16 = jnp.bfloat16
F32 = jnp.float32
SWAP = [(0, 1), (1, 0)]


def split(matrix):
    high = matrix.astype(ml_dtypes.bfloat16)
    low = (matrix - high.astype(np.float64)).astype(ml_dtypes.bfloat16)
    return high, low


@functools.cache
def transform_tables(sources):
    per_source = BASE // sources
    order = np.arange(BASE)
    a = per_source * (order % sources) + order // sources
    b = np.arange(BASE)
    k0 = np.arange(ROWS)
    live = (k0 <= BASE).astype(np.float64)[:, None]
    t0 = np.arange(64)
    t1 = np.arange(128)
    k1 = np.arange(-32, 32)
    angle = 2 * np.pi * (np.outer(k0, a) % 256) / 256
    first = np.concatenate([np.cos(angle) * live, -np.sin(angle) * live])
    first = np.concatenate(split(first), axis=1)
    angle = np.pi * np.outer(k0, 2 * b + 1) / (2 * WINDOW)
    twist = np.stack([np.cos(angle), np.sin(angle)]).astype(np.float32)
    angle_b = np.pi * (np.outer(2 * b + 1, k1) % 256) / 128
    angle_t = np.pi * (np.outer(k1, 2 * t0 + 1) % 128) / 64
    real = np.concatenate([np.cos(angle_b) @ np.cos(angle_t), np.sin(angle_b) @ np.cos(angle_t)])
    imag = np.concatenate([np.cos(angle_b) @ np.sin(angle_t), np.sin(angle_b) @ np.sin(angle_t)])
    zero = np.zeros_like(real)
    middle = np.concatenate(
        [
            np.concatenate([real, zero, imag, zero], axis=1),
            np.concatenate([zero, real, zero, imag], axis=1),
        ]
    )
    middle = np.stack(split(middle))
    weight = np.where((k0 == 0) | (k0 == BASE), 1.0 / WINDOW, 2.0 / WINDOW)[:, None] * live
    angle = np.pi * np.outer(k0, 2 * np.tile(t0, 2) + 1) / WINDOW
    untwist = np.stack([weight * np.cos(angle), weight * np.sin(angle)]).astype(np.float32)
    angle = 2 * np.pi * (np.outer(t1, k0[:BASE]) % 256) / 256
    last = np.concatenate([np.cos(angle), -np.sin(angle)], axis=1)
    last[:, BASE] = (-1.0) ** t1
    last = np.stack(split(last))
    return first, twist, middle, untwist, last


def inverse_freq():
    return jnp.exp(jnp.arange(HALF).astype(F32) * (-2.0 * math.log(THETA) / HEAD))


def pack_kernel(core_ref, mine_ref, other_ref, out_ref):
    core = core_ref[0]
    tokens = mine_ref.shape[0]
    heads, parts = 2, out_ref.shape[0] // 2
    for block_ref, place in ((mine_ref, core), (other_ref, 1 - core)):
        turned = block_ref[...].astype(F32).T
        at = pl.multiple_of(place * tokens, 128)
        for head in range(heads):
            for part in range(parts):
                low = head * HEAD + part * 8
                rows = jnp.concatenate(
                    [turned[low : low + 8], turned[low + HALF : low + HALF + 8]], axis=0
                )
                out_ref[head * parts + part, :, pl.ds(at, tokens)] = rows.astype(BF16)


def halves(block):
    high = block.astype(BF16)
    return high, (block - high.astype(F32)).astype(BF16)


def dot(left, right):
    return jnp.dot(left, right, preferred_element_type=F32)


def transform_kernel(
    x_ref, cos_ref, sin_ref, first_hbm, twist_hbm, middle_hbm, untwist_hbm, last_hbm, *refs
):
    *out_refs, first_ref, twist_ref, middle_ref, untwist_ref, last_ref, wide_ref, rows_ref, sems = refs
    copies = [
        pltpu.make_async_copy(source, target, sems.at[i])
        for i, (source, target) in enumerate(
            (
                (first_hbm, first_ref),
                (twist_hbm, twist_ref),
                (middle_hbm, middle_ref),
                (untwist_hbm, untwist_ref),
                (last_hbm, last_ref),
            )
        )
    ]
    for copy in copies:
        copy.start()
    sources, columns, run = x_ref.shape
    for source in range(sources):
        block = x_ref[source].astype(F32)
        for i in range(run // BASE):
            at = (i * sources + source) * columns
            wide_ref[pl.ds(at, columns), :] = block[:, i * BASE : i * BASE + BASE]
    pieces = [wide_ref[pl.ds(column, BASE, stride=columns), :] for column in range(columns)]
    x = jnp.concatenate(pieces, axis=1).astype(BF16)
    for copy in copies:
        copy.wait()
    cosine, sine = twist_ref[0], twist_ref[1]
    parts = []
    for pair in range(columns // 2):
        xp = x[:, pair * 256 : pair * 256 + 256]
        one = dot(first_ref[...], jnp.concatenate([xp, xp], axis=0))
        part = []
        for which in range(2):
            real = one[:ROWS, which * BASE : which * BASE + BASE]
            imag = one[ROWS:, which * BASE : which * BASE + BASE]
            part.append(real * cosine + imag * sine)
            part.append(imag * cosine - real * sine)
        parts.append(jnp.concatenate(part, axis=1))
    high, low = halves(jnp.concatenate(parts, axis=0))
    two = dot(high, middle_ref[0]) + dot(low, middle_ref[0]) + dot(high, middle_ref[1])
    top = lax.broadcasted_iota(jnp.int32, (BASE, BASE), 0) == 0
    z_real, z_imag = [], []
    for pair in range(columns // 2):
        real = two[pair * ROWS : pair * ROWS + ROWS, :BASE]
        imag = two[pair * ROWS : pair * ROWS + ROWS, BASE:]
        up = real * untwist_ref[0] - imag * untwist_ref[1]
        down = real * untwist_ref[1] + imag * untwist_ref[0]
        z_real.append(up[:BASE])
        z_imag.append(jnp.where(top, up[BASE : BASE + 1], down[:BASE]))
    z = jnp.concatenate(
        [jnp.concatenate(z_real, axis=1), jnp.concatenate(z_imag, axis=1)], axis=0
    )
    high, low = halves(z)
    y = dot(last_ref[0], high) + dot(last_ref[0], low) + dot(last_ref[1], high)
    rows_ref[...] = y.T
    steps = rows_ref.shape[0] // columns
    for step in range(steps):
        token = rows_ref[pl.ds(step, columns, stride=steps), :].astype(BF16).astype(F32)
        here = pl.ds(step * BASE, BASE)
        cosine, sine = cos_ref[:, here], sin_ref[:, here]
        up, down = token[:8], token[8:]
        turned = jnp.concatenate(
            [up * cosine - down * sine, down * cosine + up * sine], axis=0
        )
        chunk, place = divmod(step * BASE, out_refs[0].shape[1])
        out_refs[chunk][:, pl.ds(place, BASE)] = turned.astype(BF16)


def attend_rows(q, kv_ref, core, order, *, block, scale):
    _, width, tokens = kv_ref.shape
    rows = q.shape[0]
    count = tokens // block

    def scores(step):
        return dot(q, kv_ref[core, :, pl.ds(step * block, block)])

    best = jnp.full((rows, 1), -jnp.inf, F32)
    accum = jnp.zeros((rows, 2 * HEAD), F32)
    ones = jnp.ones((HEAD, block), BF16)
    upcoming = scores(0)
    for step in range(count):
        current = upcoming
        if step + 1 < count:
            upcoming = scores(step + 1)
        fresh = jnp.maximum(best, jnp.max(current, axis=1, keepdims=True))
        shrink = jnp.exp2((best - fresh) * scale)
        expo = jnp.exp2((current - fresh) * scale).astype(BF16)
        values = kv_ref[1 - core, :, pl.ds(step * block, block)]
        summed = lax.dot_general(
            expo,
            jnp.concatenate([values, ones], axis=0),
            (((1,), (1,)), ((), ())),
            preferred_element_type=F32,
        )
        accum = accum * shrink + summed
        best = fresh
    result = (accum[:, :HEAD] / accum[:, HEAD:]).astype(BF16)
    return dot(result, order).astype(BF16)


SCALE = math.log2(math.e) / math.sqrt(HEAD)
ROW_BLOCK = 768
TOKEN_BLOCK = 2048
CHUNKS = 1


def gather_attend_kernel(core_ref, q_ref, order_ref, *refs):
    *blocks, out_ref, kv_ref, sems = refs
    half = len(blocks) // 2
    columns, run = blocks[0].shape

    @pl.when(pl.program_id(0) == 0)
    def _():
        copies = []
        for i, block in enumerate(blocks):
            which, at = divmod(i, half)
            row, chunk = divmod(at, CHUNKS)
            target = kv_ref.at[which, pl.ds(row * columns, columns), pl.ds(chunk * run, run)]
            copies.append(pltpu.make_async_copy(block, target, sems.at[i]))
        for copy in copies:
            copy.start()
        for copy in copies:
            copy.wait()

    out_ref[...] = attend_rows(
        q_ref[...], kv_ref, core_ref[0], order_ref[...], block=TOKEN_BLOCK, scale=SCALE
    )


def attend_kernel(core_ref, q_ref, order_ref, kv_ref, out_ref):
    out_ref[...] = attend_rows(
        q_ref[...], kv_ref, core_ref[0], order_ref[...], block=TOKEN_BLOCK, scale=SCALE
    )


def gather_attend(core, q, order, blocks):
    rows = q.shape[0]
    columns, run = blocks[0].shape
    kv_shape = (2, len(blocks) // (2 * CHUNKS) * columns, CHUNKS * run)
    return pl.pallas_call(
        gather_attend_kernel,
        grid=(rows // ROW_BLOCK,),
        in_specs=[
            pl.BlockSpec(memory_space=pltpu.SMEM),
            pl.BlockSpec((ROW_BLOCK, HEAD), lambda i: (i, 0)),
            pl.BlockSpec(order.shape, lambda i: (0, 0)),
        ]
        + [pl.BlockSpec(memory_space=pl.ANY)] * len(blocks),
        out_specs=[
            pl.BlockSpec((ROW_BLOCK, HEAD), lambda i: (i, 0)),
            pl.BlockSpec(memory_space=pltpu.VMEM),
        ],
        out_shape=[
            jax.ShapeDtypeStruct(q.shape, BF16),
            jax.ShapeDtypeStruct(kv_shape, BF16),
        ],
        scratch_shapes=[pltpu.SemaphoreType.DMA((len(blocks),))],
        compiler_params=pltpu.CompilerParams(vmem_limit_bytes=32 * 1024 * 1024),
        name="gather_attend",
    )(core, q, order, *blocks)


def attend(core, q, order, kv):
    return pl.pallas_call(
        attend_kernel,
        grid=(q.shape[0] // ROW_BLOCK,),
        in_specs=[
            pl.BlockSpec(memory_space=pltpu.SMEM),
            pl.BlockSpec((ROW_BLOCK, HEAD), lambda i: (i, 0)),
            pl.BlockSpec(order.shape, lambda i: (0, 0)),
            pl.BlockSpec(memory_space=pltpu.VMEM),
        ],
        out_specs=pl.BlockSpec((ROW_BLOCK, HEAD), lambda i: (i, 0)),
        out_shape=jax.ShapeDtypeStruct(q.shape, BF16),
        compiler_params=pltpu.CompilerParams(vmem_limit_bytes=32 * 1024 * 1024),
        name="attend",
    )(core, q, order, kv)


def ring_gather(small, parts):
    onward = [(2 * i, 2 * ((i + 1) % parts)) for i in range(parts)]
    onward += [(2 * i + 1, 2 * ((i - 1) % parts) + 1) for i in range(parts)]

    def along(block):
        return lax.ppermute(block, ("z", "core"), onward)

    def across(block):
        return lax.ppermute(block, "core", SWAP)

    a = [along(block) for block in small]
    other = [across(block) for block in small]
    b = [along(block) for block in other]
    mine, theirs = list(small), list(other)
    for step in range(1, parts // 2):
        a_next = [along(block) for block in a]
        a_swapped = [across(block) for block in a]
        b_next = [along(block) for block in b] if step + 1 < parts // 2 else None
        b_swapped = [across(block) for block in b]
        mine += a + b_swapped
        theirs += b + a_swapped
        a, b = a_next, b_next
    return mine + a, theirs + [across(block) for block in a]


def on_device(keys, values, queries, positions):
    core = lax.axis_index("core")
    head = lax.axis_index("yhi")
    place = lax.axis_index("z")
    parts = lax.axis_size("z")
    sources = 2 * parts
    tokens = keys.shape[0]
    core_here = core[None].astype(jnp.int32)

    vmem = pl.BlockSpec(memory_space=pltpu.VMEM)
    smem = pl.BlockSpec(memory_space=pltpu.SMEM)
    hbm = pl.BlockSpec(memory_space=pltpu.HBM)
    kept_tokens = jnp.where(core == 0, keys, values)
    send = jnp.where(core == 0, values, keys)
    kept_tokens, send = lax.optimization_barrier((kept_tokens, send))
    other = lax.ppermute(send, "core", SWAP)
    packed = pl.pallas_call(
        pack_kernel,
        in_specs=[smem, vmem, vmem],
        out_specs=vmem,
        out_shape=jax.ShapeDtypeStruct((sources, COLUMNS, 2 * tokens), BF16),
        compiler_params=pltpu.CompilerParams(vmem_limit_bytes=16 * 1024 * 1024),
        name="pack",
    )(core_here, kept_tokens, other)
    places_here = positions.astype(F32)
    packed, queries, places_here = lax.optimization_barrier((packed, queries, places_here))
    received = lax.all_to_all(packed, ("yhi", "z"), 0, 0, tiled=True)

    freq = inverse_freq()
    angles = places_here[:, None] * freq[None, :]
    cosine, sine = jnp.cos(angles), jnp.sin(angles)
    wide = queries.astype(F32)
    up, down = wide[..., :HALF], wide[..., HALF:]
    turned = jnp.concatenate(
        [up * cosine - down * sine, down * cosine + up * sine], axis=-1
    ).astype(BF16)
    lane = jnp.arange(HEAD)
    at = lane // COLUMNS
    away = jnp.where(at % 2 == 1, -1, 1) * ((at + 1) // 2) * jnp.where(core == 0, 1, -1)
    owner = (place + away) % parts
    column = ((lane % COLUMNS) // 8) * HALF + owner * 8 + lane % 8
    order = (lane[:, None] == column[None, :]).astype(BF16)
    turned = jnp.einsum("hqd,de->hqe", turned, order, preferred_element_type=F32).astype(BF16)
    own = jnp.where(head == 0, turned[0], turned[1])
    guest = lax.ppermute(jnp.where(head == 0, turned[1], turned[0]), "yhi", SWAP)

    index = jnp.arange(KEPT)
    places = (64 * (index % BASE) + index // BASE).astype(F32)
    angles = lax.dynamic_slice(freq, (8 * place,), (8,))[:, None] * places[None, :]
    cosine = jnp.where(core == 0, jnp.cos(angles), 1.0)
    sine = jnp.where(core == 0, jnp.sin(angles), 0.0)
    received, own, guest, cosine, sine = lax.optimization_barrier(
        (received, own, guest, cosine, sine)
    )
    tables = transform_tables(sources)
    small = pl.pallas_call(
        transform_kernel,
        in_specs=[vmem] * 3 + [hbm] * 5,
        out_specs=[vmem] * CHUNKS,
        out_shape=[jax.ShapeDtypeStruct((COLUMNS, KEPT // CHUNKS), BF16)] * CHUNKS,
        scratch_shapes=[pltpu.VMEM(t.shape, t.dtype) for t in tables]
        + [
            pltpu.VMEM((BASE * COLUMNS, BASE), F32),
            pltpu.VMEM((64 * COLUMNS, BASE), F32),
            pltpu.SemaphoreType.DMA((len(tables),)),
        ],
        compiler_params=pltpu.CompilerParams(vmem_limit_bytes=32 * 1024 * 1024),
        name="transform",
    )(received, cosine, sine, *map(jnp.asarray, tables))

    mine, theirs = ring_gather(small, parts)
    back = order.T
    first, kv = gather_attend(core_here, guest, back, mine + theirs)
    returned = lax.ppermute(first, "yhi", SWAP)
    kept = attend(core_here, own, back, kv)
    return jnp.where(
        head == 0, jnp.stack([kept, returned]), jnp.stack([returned, kept])
    )


def solution(mesh):
    shape = mesh.devices.shape
    fine = Mesh(
        mesh.devices.reshape(shape[0], shape[1], 2, shape[2] // 4, 2),
        ("user", "heads", "yhi", "z", "core"),
    )
    tokens = ("user", "yhi", "z", "core")
    return jax.shard_map(
        on_device,
        mesh=fine,
        in_specs=(P(tokens, "heads"), P(tokens, "heads"), P("heads", tokens, None), P(tokens)),
        out_specs=P("heads", tokens, None),
        check_vma=False,
    )
```

```python
import functools
import math

import jax
import jax.numpy as jnp
import ml_dtypes
import numpy as np
from jax import lax
from jax.experimental import pallas as pl
from jax.experimental.pallas import tpu as pltpu
from jax.sharding import Mesh
from jax.sharding import PartitionSpec as P

WINDOW = 16384
KEPT = WINDOW // 2
HEAD = 128
HALF = HEAD // 2
COLUMNS = 16
BASE = 128
ROWS = 136
THETA = 500000.0
BF16 = jnp.bfloat16
F32 = jnp.float32
SWAP = [(0, 1), (1, 0)]


def split(matrix):
    high = matrix.astype(ml_dtypes.bfloat16)
    low = (matrix - high.astype(np.float64)).astype(ml_dtypes.bfloat16)
    return high, low


@functools.cache
def transform_tables(sources):
    per_source = BASE // sources
    order = np.arange(BASE)
    a = per_source * (order % sources) + order // sources
    b = np.arange(BASE)
    k0 = np.arange(ROWS)
    live = (k0 <= BASE).astype(np.float64)[:, None]
    t0 = np.arange(64)
    t1 = np.arange(128)
    k1 = np.arange(-32, 32)
    angle = 2 * np.pi * (np.outer(k0, a) % 256) / 256
    first = np.concatenate([np.cos(angle) * live, -np.sin(angle) * live])
    first = np.concatenate(split(first), axis=1)
    angle = np.pi * np.outer(k0, 2 * b + 1) / (2 * WINDOW)
    twist = np.stack([np.cos(angle), np.sin(angle)]).astype(np.float32)
    angle_b = np.pi * (np.outer(2 * b + 1, k1) % 256) / 128
    angle_t = np.pi * (np.outer(k1, 2 * t0 + 1) % 128) / 64
    real = np.concatenate([np.cos(angle_b) @ np.cos(angle_t), np.sin(angle_b) @ np.cos(angle_t)])
    imag = np.concatenate([np.cos(angle_b) @ np.sin(angle_t), np.sin(angle_b) @ np.sin(angle_t)])
    zero = np.zeros_like(real)
    middle = np.concatenate(
        [
            np.concatenate([real, zero, imag, zero], axis=1),
            np.concatenate([zero, real, zero, imag], axis=1),
        ]
    )
    middle = np.stack(split(middle))
    weight = np.where((k0 == 0) | (k0 == BASE), 1.0 / WINDOW, 2.0 / WINDOW)[:, None] * live
    angle = np.pi * np.outer(k0, 2 * np.tile(t0, 2) + 1) / WINDOW
    untwist = np.stack([weight * np.cos(angle), weight * np.sin(angle)]).astype(np.float32)
    angle = 2 * np.pi * (np.outer(t1, k0[:BASE]) % 256) / 256
    last = np.concatenate([np.cos(angle), -np.sin(angle)], axis=1)
    last[:, BASE] = (-1.0) ** t1
    last = np.stack(split(last))
    return first, twist, middle, untwist, last


def inverse_freq():
    return jnp.exp(jnp.arange(HALF).astype(F32) * (-2.0 * math.log(THETA) / HEAD))


def pack_kernel(core_ref, mine_ref, other_ref, out_ref):
    core = core_ref[0]
    tokens = mine_ref.shape[0]
    heads, parts = 2, out_ref.shape[0] // 2
    for block_ref, place in ((mine_ref, core), (other_ref, 1 - core)):
        turned = block_ref[...].astype(F32).T
        at = pl.multiple_of(place * tokens, 128)
        for head in range(heads):
            for part in range(parts):
                low = head * HEAD + part * 8
                rows = jnp.concatenate(
                    [turned[low : low + 8], turned[low + HALF : low + HALF + 8]], axis=0
                )
                out_ref[head * parts + part, :, pl.ds(at, tokens)] = rows.astype(BF16)


def halves(block):
    high = block.astype(BF16)
    return high, (block - high.astype(F32)).astype(BF16)


def dot(left, right):
    return jnp.dot(left, right, preferred_element_type=F32)


def transform_kernel(
    x_ref, cos_ref, sin_ref, first_hbm, twist_hbm, middle_hbm, untwist_hbm, last_hbm, *refs
):
    *out_refs, first_ref, twist_ref, middle_ref, untwist_ref, last_ref, wide_ref, rows_ref, sems = refs
    copies = [
        pltpu.make_async_copy(source, target, sems.at[i])
        for i, (source, target) in enumerate(
            (
                (first_hbm, first_ref),
                (twist_hbm, twist_ref),
                (middle_hbm, middle_ref),
                (untwist_hbm, untwist_ref),
                (last_hbm, last_ref),
            )
        )
    ]
    for copy in copies:
        copy.start()
    sources, columns, run = x_ref.shape
    for source in range(sources):
        block = x_ref[source].astype(F32)
        for i in range(run // BASE):
            at = (i * sources + source) * columns
            wide_ref[pl.ds(at, columns), :] = block[:, i * BASE : i * BASE + BASE]
    pieces = [wide_ref[pl.ds(column, BASE, stride=columns), :] for column in range(columns)]
    x = jnp.concatenate(pieces, axis=1).astype(BF16)
    for copy in copies:
        copy.wait()
    cosine, sine = twist_ref[0], twist_ref[1]
    parts = []
    for pair in range(columns // 2):
        xp = x[:, pair * 256 : pair * 256 + 256]
        one = dot(first_ref[...], jnp.concatenate([xp, xp], axis=0))
        part = []
        for which in range(2):
            real = one[:ROWS, which * BASE : which * BASE + BASE]
            imag = one[ROWS:, which * BASE : which * BASE + BASE]
            part.append(real * cosine + imag * sine)
            part.append(imag * cosine - real * sine)
        parts.append(jnp.concatenate(part, axis=1))
    high, low = halves(jnp.concatenate(parts, axis=0))
    two = dot(high, middle_ref[0]) + dot(low, middle_ref[0]) + dot(high, middle_ref[1])
    top = lax.broadcasted_iota(jnp.int32, (BASE, BASE), 0) == 0
    z_real, z_imag = [], []
    for pair in range(columns // 2):
        real = two[pair * ROWS : pair * ROWS + ROWS, :BASE]
        imag = two[pair * ROWS : pair * ROWS + ROWS, BASE:]
        up = real * untwist_ref[0] - imag * untwist_ref[1]
        down = real * untwist_ref[1] + imag * untwist_ref[0]
        z_real.append(up[:BASE])
        z_imag.append(jnp.where(top, up[BASE : BASE + 1], down[:BASE]))
    z = jnp.concatenate(
        [jnp.concatenate(z_real, axis=1), jnp.concatenate(z_imag, axis=1)], axis=0
    )
    high, low = halves(z)
    both = dot(jnp.concatenate([last_ref[0], last_ref[1]], axis=0), high)
    y = both[:BASE] + both[BASE:] + dot(last_ref[0], low)
    rows_ref[...] = y.T
    steps = rows_ref.shape[0] // columns
    for step in range(steps):
        token = rows_ref[pl.ds(step, columns, stride=steps), :].astype(BF16).astype(F32)
        here = pl.ds(step * BASE, BASE)
        cosine, sine = cos_ref[:, here], sin_ref[:, here]
        up, down = token[:8], token[8:]
        turned = jnp.concatenate(
            [up * cosine - down * sine, down * cosine + up * sine], axis=0
        )
        chunk, place = divmod(step * BASE, out_refs[0].shape[1])
        out_refs[chunk][:, pl.ds(place, BASE)] = turned.astype(BF16)


def attend_rows(q, kv_ref, core, order, *, block, scale):
    _, width, tokens = kv_ref.shape
    rows = q.shape[0]
    count = tokens // block

    def scores(step):
        return dot(q, kv_ref[core, :, pl.ds(step * block, block)])

    best = jnp.full((rows, 1), -jnp.inf, F32)
    accum = jnp.zeros((rows, 2 * HEAD), F32)
    ones = jnp.ones((HEAD, block), BF16)
    upcoming = scores(0)
    for step in range(count):
        current = upcoming
        if step + 1 < count:
            upcoming = scores(step + 1)
        fresh = jnp.maximum(best, jnp.max(current, axis=1, keepdims=True))
        shrink = jnp.exp2((best - fresh) * scale)
        expo = jnp.exp2((current - fresh) * scale).astype(BF16)
        values = kv_ref[1 - core, :, pl.ds(step * block, block)]
        summed = lax.dot_general(
            expo,
            jnp.concatenate([values, ones], axis=0),
            (((1,), (1,)), ((), ())),
            preferred_element_type=F32,
        )
        accum = accum * shrink + summed
        best = fresh
    result = (accum[:, :HEAD] / accum[:, HEAD:]).astype(BF16)
    return dot(result, order).astype(BF16)


SCALE = math.log2(math.e) / math.sqrt(HEAD)
ROW_BLOCK = 768
TOKEN_BLOCK = 2048
CHUNKS = 1


def gather_attend_kernel(core_ref, q_ref, order_ref, *refs):
    *blocks, out_ref, kv_ref = refs
    half = len(blocks) // 2
    columns, run = blocks[0].shape

    @pl.when(pl.program_id(0) == 0)
    def _():
        for i, block in enumerate(blocks):
            which, at = divmod(i, half)
            row, chunk = divmod(at, CHUNKS)
            kv_ref[which, pl.ds(row * columns, columns), pl.ds(chunk * run, run)] = block[...]

    out_ref[...] = attend_rows(
        q_ref[...], kv_ref, core_ref[0], order_ref[...], block=TOKEN_BLOCK, scale=SCALE
    )


def attend_kernel(core_ref, q_ref, order_ref, kv_ref, out_ref):
    out_ref[...] = attend_rows(
        q_ref[...], kv_ref, core_ref[0], order_ref[...], block=TOKEN_BLOCK, scale=SCALE
    )


def gather_attend(core, q, order, blocks):
    rows = q.shape[0]
    columns, run = blocks[0].shape
    kv_shape = (2, len(blocks) // (2 * CHUNKS) * columns, CHUNKS * run)
    return pl.pallas_call(
        gather_attend_kernel,
        grid=(rows // ROW_BLOCK,),
        in_specs=[
            pl.BlockSpec(memory_space=pltpu.SMEM),
            pl.BlockSpec((ROW_BLOCK, HEAD), lambda i: (i, 0)),
            pl.BlockSpec(order.shape, lambda i: (0, 0)),
        ]
        + [pl.BlockSpec(memory_space=pltpu.VMEM)] * len(blocks),
        out_specs=[
            pl.BlockSpec((ROW_BLOCK, HEAD), lambda i: (i, 0)),
            pl.BlockSpec(memory_space=pltpu.VMEM),
        ],
        out_shape=[
            jax.ShapeDtypeStruct(q.shape, BF16),
            jax.ShapeDtypeStruct(kv_shape, BF16),
        ],
        compiler_params=pltpu.CompilerParams(vmem_limit_bytes=32 * 1024 * 1024),
        name="gather_attend",
    )(core, q, order, *blocks)


def attend(core, q, order, kv):
    return pl.pallas_call(
        attend_kernel,
        grid=(q.shape[0] // ROW_BLOCK,),
        in_specs=[
            pl.BlockSpec(memory_space=pltpu.SMEM),
            pl.BlockSpec((ROW_BLOCK, HEAD), lambda i: (i, 0)),
            pl.BlockSpec(order.shape, lambda i: (0, 0)),
            pl.BlockSpec(memory_space=pltpu.VMEM),
        ],
        out_specs=pl.BlockSpec((ROW_BLOCK, HEAD), lambda i: (i, 0)),
        out_shape=jax.ShapeDtypeStruct(q.shape, BF16),
        compiler_params=pltpu.CompilerParams(vmem_limit_bytes=32 * 1024 * 1024),
        name="attend",
    )(core, q, order, kv)


def ring_gather(small, parts):
    onward = [(2 * i, 2 * ((i + 1) % parts)) for i in range(parts)]
    onward += [(2 * i + 1, 2 * ((i - 1) % parts) + 1) for i in range(parts)]

    def along(block):
        return lax.ppermute(block, ("z", "core"), onward)

    def across(block):
        return lax.ppermute(block, "core", SWAP)

    a = [along(block) for block in small]
    other = [across(block) for block in small]
    b = [along(block) for block in other]
    mine, theirs = list(small), list(other)
    for step in range(1, parts // 2):
        a_next = [along(block) for block in a]
        a_swapped = [across(block) for block in a]
        b_next = [along(block) for block in b] if step + 1 < parts // 2 else None
        b_swapped = [across(block) for block in b]
        mine += a + b_swapped
        theirs += b + a_swapped
        a, b = a_next, b_next
    return mine + a, theirs + [across(block) for block in a]


def on_device(keys, values, queries, positions):
    core = lax.axis_index("core")
    head = lax.axis_index("yhi")
    place = lax.axis_index("z")
    parts = lax.axis_size("z")
    sources = 2 * parts
    tokens = keys.shape[0]
    core_here = core[None].astype(jnp.int32)

    vmem = pl.BlockSpec(memory_space=pltpu.VMEM)
    smem = pl.BlockSpec(memory_space=pltpu.SMEM)
    hbm = pl.BlockSpec(memory_space=pltpu.HBM)
    kept_tokens = jnp.where(core == 0, keys, values)
    send = jnp.where(core == 0, values, keys)
    kept_tokens, send = lax.optimization_barrier((kept_tokens, send))
    other = lax.ppermute(send, "core", SWAP)
    packed = pl.pallas_call(
        pack_kernel,
        in_specs=[smem, vmem, vmem],
        out_specs=vmem,
        out_shape=jax.ShapeDtypeStruct((sources, COLUMNS, 2 * tokens), BF16),
        compiler_params=pltpu.CompilerParams(vmem_limit_bytes=16 * 1024 * 1024),
        name="pack",
    )(core_here, kept_tokens, other)
    places_here = positions.astype(F32)
    packed, queries, places_here = lax.optimization_barrier((packed, queries, places_here))
    received = lax.all_to_all(packed, ("yhi", "z"), 0, 0, tiled=True)

    freq = inverse_freq()
    angles = places_here[:, None] * freq[None, :]
    cosine, sine = jnp.cos(angles), jnp.sin(angles)
    wide = queries.astype(F32)
    up, down = wide[..., :HALF], wide[..., HALF:]
    turned = jnp.concatenate(
        [up * cosine - down * sine, down * cosine + up * sine], axis=-1
    ).astype(BF16)
    lane = jnp.arange(HEAD)
    at = lane // COLUMNS
    away = jnp.where(at % 2 == 1, -1, 1) * ((at + 1) // 2) * jnp.where(core == 0, 1, -1)
    owner = (place + away) % parts
    column = ((lane % COLUMNS) // 8) * HALF + owner * 8 + lane % 8
    order = (lane[:, None] == column[None, :]).astype(BF16)
    turned = jnp.einsum("hqd,de->hqe", turned, order, preferred_element_type=F32).astype(BF16)
    own = jnp.where(head == 0, turned[0], turned[1])
    guest = lax.ppermute(jnp.where(head == 0, turned[1], turned[0]), "yhi", SWAP)

    index = jnp.arange(KEPT)
    places = (64 * (index % BASE) + index // BASE).astype(F32)
    angles = lax.dynamic_slice(freq, (8 * place,), (8,))[:, None] * places[None, :]
    cosine = jnp.where(core == 0, jnp.cos(angles), 1.0)
    sine = jnp.where(core == 0, jnp.sin(angles), 0.0)
    received, own, guest, cosine, sine = lax.optimization_barrier(
        (received, own, guest, cosine, sine)
    )
    tables = transform_tables(sources)
    small = pl.pallas_call(
        transform_kernel,
        in_specs=[vmem] * 3 + [hbm] * 5,
        out_specs=[vmem] * CHUNKS,
        out_shape=[jax.ShapeDtypeStruct((COLUMNS, KEPT // CHUNKS), BF16)] * CHUNKS,
        scratch_shapes=[pltpu.VMEM(t.shape, t.dtype) for t in tables]
        + [
            pltpu.VMEM((BASE * COLUMNS, BASE), F32),
            pltpu.VMEM((64 * COLUMNS, BASE), F32),
            pltpu.SemaphoreType.DMA((len(tables),)),
        ],
        compiler_params=pltpu.CompilerParams(vmem_limit_bytes=32 * 1024 * 1024),
        name="transform",
    )(received, cosine, sine, *map(jnp.asarray, tables))

    mine, theirs = ring_gather(small, parts)
    back = order.T
    first, kv = gather_attend(core_here, guest, back, mine + theirs)
    returned = lax.ppermute(first, "yhi", SWAP)
    kept = attend(core_here, own, back, kv)
    return jnp.where(
        head == 0, jnp.stack([kept, returned]), jnp.stack([returned, kept])
    )


def solution(mesh):
    shape = mesh.devices.shape
    fine = Mesh(
        mesh.devices.reshape(shape[0], shape[1], 2, shape[2] // 4, 2),
        ("user", "heads", "yhi", "z", "core"),
    )
    tokens = ("user", "yhi", "z", "core")
    return jax.shard_map(
        on_device,
        mesh=fine,
        in_specs=(P(tokens, "heads"), P(tokens, "heads"), P("heads", tokens, None), P(tokens)),
        out_specs=P("heads", tokens, None),
        check_vma=False,
    )
```

```python
import functools
import math

import jax
import jax.numpy as jnp
import ml_dtypes
import numpy as np
from jax import lax
from jax.experimental import pallas as pl
from jax.experimental.pallas import tpu as pltpu
from jax.sharding import Mesh
from jax.sharding import PartitionSpec as P

WINDOW = 16384
KEPT = WINDOW // 2
HEAD = 128
HALF = HEAD // 2
COLUMNS = 16
BASE = 128
ROWS = 136
THETA = 500000.0
BF16 = jnp.bfloat16
F32 = jnp.float32
SWAP = [(0, 1), (1, 0)]


def split(matrix):
    high = matrix.astype(ml_dtypes.bfloat16)
    low = (matrix - high.astype(np.float64)).astype(ml_dtypes.bfloat16)
    return high, low


@functools.cache
def transform_tables(sources):
    per_source = BASE // sources
    order = np.arange(BASE)
    a = per_source * (order % sources) + order // sources
    b = np.arange(BASE)
    k0 = np.arange(ROWS)
    live = (k0 <= BASE).astype(np.float64)[:, None]
    t0 = np.arange(64)
    t1 = np.arange(128)
    k1 = np.arange(-32, 32)
    angle = 2 * np.pi * (np.outer(k0, a) % 256) / 256
    first = np.concatenate([np.cos(angle) * live, -np.sin(angle) * live])
    first = np.concatenate(split(first), axis=1)
    angle = np.pi * np.outer(k0, 2 * b + 1) / (2 * WINDOW)
    twist = np.stack([np.cos(angle), np.sin(angle)]).astype(np.float32)
    angle_b = np.pi * (np.outer(2 * b + 1, k1) % 256) / 128
    angle_t = np.pi * (np.outer(k1, 2 * t0 + 1) % 128) / 64
    real = np.concatenate([np.cos(angle_b) @ np.cos(angle_t), np.sin(angle_b) @ np.cos(angle_t)])
    imag = np.concatenate([np.cos(angle_b) @ np.sin(angle_t), np.sin(angle_b) @ np.sin(angle_t)])
    zero = np.zeros_like(real)
    middle = np.concatenate(
        [
            np.concatenate([real, zero, imag, zero], axis=1),
            np.concatenate([zero, real, zero, imag], axis=1),
        ]
    )
    middle = np.stack(split(middle))
    weight = np.where((k0 == 0) | (k0 == BASE), 1.0 / WINDOW, 2.0 / WINDOW)[:, None] * live
    angle = np.pi * np.outer(k0, 2 * np.tile(t0, 2) + 1) / WINDOW
    untwist = np.stack([weight * np.cos(angle), weight * np.sin(angle)]).astype(np.float32)
    angle = 2 * np.pi * (np.outer(t1, k0[:BASE]) % 256) / 256
    last = np.concatenate([np.cos(angle), -np.sin(angle)], axis=1)
    last[:, BASE] = (-1.0) ** t1
    last = np.stack(split(last))
    return first, twist, middle, untwist, last


def inverse_freq():
    return jnp.exp(jnp.arange(HALF).astype(F32) * (-2.0 * math.log(THETA) / HEAD))


def turn(block_ref, store):
    turned = block_ref[...].astype(F32).T
    parts = turned.shape[0] // COLUMNS
    for part in range(parts):
        low = part // (parts // 2) * HEAD + part % (parts // 2) * 8
        rows = jnp.concatenate([turned[low : low + 8], turned[low + HALF : low + HALF + 8]], axis=0)
        store(part, rows.astype(BF16))


def turn_kernel(mine_ref, out_ref):
    def store(part, rows):
        out_ref[part] = rows

    turn(mine_ref, store)


def pack_kernel(core_ref, turned_ref, other_ref, out_ref):
    core = core_ref[0]
    tokens = other_ref.shape[0]
    here = pl.multiple_of(core * tokens, 128)
    there = pl.multiple_of((1 - core) * tokens, 128)
    out_ref[:, :, pl.ds(here, tokens)] = turned_ref[...]

    def store(part, rows):
        out_ref[part, :, pl.ds(there, tokens)] = rows

    turn(other_ref, store)


def halves(block):
    high = block.astype(BF16)
    return high, (block - high.astype(F32)).astype(BF16)


def dot(left, right):
    return jnp.dot(left, right, preferred_element_type=F32)


def transform_kernel(
    x_ref, cos_ref, sin_ref, first_hbm, twist_hbm, middle_hbm, untwist_hbm, last_hbm, *refs
):
    *out_refs, first_ref, twist_ref, middle_ref, untwist_ref, last_ref, wide_ref, rows_ref, sems = refs
    copies = [
        pltpu.make_async_copy(source, target, sems.at[i])
        for i, (source, target) in enumerate(
            (
                (first_hbm, first_ref),
                (twist_hbm, twist_ref),
                (middle_hbm, middle_ref),
                (untwist_hbm, untwist_ref),
                (last_hbm, last_ref),
            )
        )
    ]
    for copy in copies:
        copy.start()
    sources, columns, run = x_ref.shape
    for source in range(sources):
        block = x_ref[source].astype(F32)
        for i in range(run // BASE):
            at = (i * sources + source) * columns
            wide_ref[pl.ds(at, columns), :] = block[:, i * BASE : i * BASE + BASE]
    pieces = [wide_ref[pl.ds(column, BASE, stride=columns), :] for column in range(columns)]
    x = jnp.concatenate(pieces, axis=1).astype(BF16)
    for copy in copies:
        copy.wait()
    cosine, sine = twist_ref[0], twist_ref[1]
    parts = []
    for pair in range(columns // 2):
        xp = x[:, pair * 256 : pair * 256 + 256]
        one = dot(first_ref[...], jnp.concatenate([xp, xp], axis=0))
        part = []
        for which in range(2):
            real = one[:ROWS, which * BASE : which * BASE + BASE]
            imag = one[ROWS:, which * BASE : which * BASE + BASE]
            part.append(real * cosine + imag * sine)
            part.append(imag * cosine - real * sine)
        parts.append(jnp.concatenate(part, axis=1))
    high, low = halves(jnp.concatenate(parts, axis=0))
    two = dot(high, middle_ref[0]) + dot(low, middle_ref[0]) + dot(high, middle_ref[1])
    top = lax.broadcasted_iota(jnp.int32, (BASE, BASE), 0) == 0
    z_real, z_imag = [], []
    for pair in range(columns // 2):
        real = two[pair * ROWS : pair * ROWS + ROWS, :BASE]
        imag = two[pair * ROWS : pair * ROWS + ROWS, BASE:]
        up = real * untwist_ref[0] - imag * untwist_ref[1]
        down = real * untwist_ref[1] + imag * untwist_ref[0]
        z_real.append(up[:BASE])
        z_imag.append(jnp.where(top, up[BASE : BASE + 1], down[:BASE]))
    z = jnp.concatenate(
        [jnp.concatenate(z_real, axis=1), jnp.concatenate(z_imag, axis=1)], axis=0
    )
    high, low = halves(z)
    both = dot(jnp.concatenate([last_ref[0], last_ref[1]], axis=0), high)
    y = both[:BASE] + both[BASE:] + dot(last_ref[0], low)
    rows_ref[...] = y.T
    steps = rows_ref.shape[0] // columns
    for step in range(steps):
        token = rows_ref[pl.ds(step, columns, stride=steps), :].astype(BF16).astype(F32)
        here = pl.ds(step * BASE, BASE)
        cosine, sine = cos_ref[:, here], sin_ref[:, here]
        up, down = token[:8], token[8:]
        turned = jnp.concatenate(
            [up * cosine - down * sine, down * cosine + up * sine], axis=0
        )
        chunk, place = divmod(step * BASE, out_refs[0].shape[1])
        out_refs[chunk][:, pl.ds(place, BASE)] = turned.astype(BF16)


def attend_rows(q, kv_ref, core, order, *, block, scale):
    _, width, tokens = kv_ref.shape
    rows = q.shape[0]
    count = tokens // block

    def scores(step):
        return dot(q, kv_ref[core, :, pl.ds(step * block, block)])

    best = jnp.full((rows, 1), -jnp.inf, F32)
    accum = jnp.zeros((rows, 2 * HEAD), F32)
    ones = jnp.ones((HEAD, block), BF16)
    upcoming = scores(0)
    for step in range(count):
        current = upcoming
        if step + 1 < count:
            upcoming = scores(step + 1)
        fresh = jnp.maximum(best, jnp.max(current, axis=1, keepdims=True))
        shrink = jnp.exp2((best - fresh) * scale)
        expo = jnp.exp2((current - fresh) * scale).astype(BF16)
        values = kv_ref[1 - core, :, pl.ds(step * block, block)]
        summed = lax.dot_general(
            expo,
            jnp.concatenate([values, ones], axis=0),
            (((1,), (1,)), ((), ())),
            preferred_element_type=F32,
        )
        accum = accum * shrink + summed
        best = fresh
    result = (accum[:, :HEAD] / accum[:, HEAD:]).astype(BF16)
    return dot(result, order).astype(BF16)


SCALE = math.log2(math.e) / math.sqrt(HEAD)
ROW_BLOCK = 768
TOKEN_BLOCK = 2048
CHUNKS = 1


def gather_attend_kernel(core_ref, q_ref, order_ref, *refs):
    *blocks, out_ref, kv_ref = refs
    half = len(blocks) // 2
    columns, run = blocks[0].shape

    @pl.when(pl.program_id(0) == 0)
    def _():
        for i, block in enumerate(blocks):
            which, at = divmod(i, half)
            row, chunk = divmod(at, CHUNKS)
            kv_ref[which, pl.ds(row * columns, columns), pl.ds(chunk * run, run)] = block[...]

    out_ref[...] = attend_rows(
        q_ref[...], kv_ref, core_ref[0], order_ref[...], block=TOKEN_BLOCK, scale=SCALE
    )


def attend_kernel(core_ref, q_ref, order_ref, kv_ref, out_ref):
    out_ref[...] = attend_rows(
        q_ref[...], kv_ref, core_ref[0], order_ref[...], block=TOKEN_BLOCK, scale=SCALE
    )


def gather_attend(core, q, order, blocks):
    rows = q.shape[0]
    columns, run = blocks[0].shape
    kv_shape = (2, len(blocks) // (2 * CHUNKS) * columns, CHUNKS * run)
    return pl.pallas_call(
        gather_attend_kernel,
        grid=(rows // ROW_BLOCK,),
        in_specs=[
            pl.BlockSpec(memory_space=pltpu.SMEM),
            pl.BlockSpec((ROW_BLOCK, HEAD), lambda i: (i, 0)),
            pl.BlockSpec(order.shape, lambda i: (0, 0)),
        ]
        + [pl.BlockSpec(memory_space=pltpu.VMEM)] * len(blocks),
        out_specs=[
            pl.BlockSpec((ROW_BLOCK, HEAD), lambda i: (i, 0)),
            pl.BlockSpec(memory_space=pltpu.VMEM),
        ],
        out_shape=[
            jax.ShapeDtypeStruct(q.shape, BF16),
            jax.ShapeDtypeStruct(kv_shape, BF16),
        ],
        compiler_params=pltpu.CompilerParams(vmem_limit_bytes=32 * 1024 * 1024),
        name="gather_attend",
    )(core, q, order, *blocks)


def attend(core, q, order, kv):
    return pl.pallas_call(
        attend_kernel,
        grid=(q.shape[0] // ROW_BLOCK,),
        in_specs=[
            pl.BlockSpec(memory_space=pltpu.SMEM),
            pl.BlockSpec((ROW_BLOCK, HEAD), lambda i: (i, 0)),
            pl.BlockSpec(order.shape, lambda i: (0, 0)),
            pl.BlockSpec(memory_space=pltpu.VMEM),
        ],
        out_specs=pl.BlockSpec((ROW_BLOCK, HEAD), lambda i: (i, 0)),
        out_shape=jax.ShapeDtypeStruct(q.shape, BF16),
        compiler_params=pltpu.CompilerParams(vmem_limit_bytes=32 * 1024 * 1024),
        name="attend",
    )(core, q, order, kv)


def ring_gather(small, parts):
    onward = [(2 * i, 2 * ((i + 1) % parts)) for i in range(parts)]
    onward += [(2 * i + 1, 2 * ((i - 1) % parts) + 1) for i in range(parts)]

    def along(block):
        return lax.ppermute(block, ("z", "core"), onward)

    def across(block):
        return lax.ppermute(block, "core", SWAP)

    a = [along(block) for block in small]
    other = [across(block) for block in small]
    b = [along(block) for block in other]
    mine, theirs = list(small), list(other)
    for step in range(1, parts // 2):
        a_next = [along(block) for block in a]
        a_swapped = [across(block) for block in a]
        b_next = [along(block) for block in b] if step + 1 < parts // 2 else None
        b_swapped = [across(block) for block in b]
        mine += a + b_swapped
        theirs += b + a_swapped
        a, b = a_next, b_next
    return mine + a, theirs + [across(block) for block in a]


def on_device(keys, values, queries, positions):
    core = lax.axis_index("core")
    head = lax.axis_index("yhi")
    place = lax.axis_index("z")
    parts = lax.axis_size("z")
    sources = 2 * parts
    tokens = keys.shape[0]
    core_here = core[None].astype(jnp.int32)

    vmem = pl.BlockSpec(memory_space=pltpu.VMEM)
    smem = pl.BlockSpec(memory_space=pltpu.SMEM)
    hbm = pl.BlockSpec(memory_space=pltpu.HBM)
    kept_tokens = jnp.where(core == 0, keys, values)
    send = jnp.where(core == 0, values, keys)
    kept_tokens, send = lax.optimization_barrier((kept_tokens, send))
    other = lax.ppermute(send, "core", SWAP)
    turned_tokens = pl.pallas_call(
        turn_kernel,
        in_specs=[vmem],
        out_specs=vmem,
        out_shape=jax.ShapeDtypeStruct((sources, COLUMNS, tokens), BF16),
        compiler_params=pltpu.CompilerParams(vmem_limit_bytes=16 * 1024 * 1024),
        name="turn",
    )(kept_tokens)
    packed = pl.pallas_call(
        pack_kernel,
        in_specs=[smem, vmem, vmem],
        out_specs=vmem,
        out_shape=jax.ShapeDtypeStruct((sources, COLUMNS, 2 * tokens), BF16),
        compiler_params=pltpu.CompilerParams(vmem_limit_bytes=16 * 1024 * 1024),
        name="pack",
    )(core_here, turned_tokens, other)
    places_here = positions.astype(F32)
    packed, queries, places_here = lax.optimization_barrier((packed, queries, places_here))
    received = lax.all_to_all(packed, ("yhi", "z"), 0, 0, tiled=True)

    freq = inverse_freq()
    angles = places_here[:, None] * freq[None, :]
    cosine, sine = jnp.cos(angles), jnp.sin(angles)
    wide = queries.astype(F32)
    up, down = wide[..., :HALF], wide[..., HALF:]
    turned = jnp.concatenate(
        [up * cosine - down * sine, down * cosine + up * sine], axis=-1
    ).astype(BF16)
    lane = jnp.arange(HEAD)
    at = lane // COLUMNS
    away = jnp.where(at % 2 == 1, -1, 1) * ((at + 1) // 2) * jnp.where(core == 0, 1, -1)
    owner = (place + away) % parts
    column = ((lane % COLUMNS) // 8) * HALF + owner * 8 + lane % 8
    order = (lane[:, None] == column[None, :]).astype(BF16)
    turned = jnp.einsum("hqd,de->hqe", turned, order, preferred_element_type=F32).astype(BF16)
    own = jnp.where(head == 0, turned[0], turned[1])
    guest = lax.ppermute(jnp.where(head == 0, turned[1], turned[0]), "yhi", SWAP)

    index = jnp.arange(KEPT)
    places = (64 * (index % BASE) + index // BASE).astype(F32)
    angles = lax.dynamic_slice(freq, (8 * place,), (8,))[:, None] * places[None, :]
    cosine = jnp.where(core == 0, jnp.cos(angles), 1.0)
    sine = jnp.where(core == 0, jnp.sin(angles), 0.0)
    received, own, guest, cosine, sine = lax.optimization_barrier(
        (received, own, guest, cosine, sine)
    )
    tables = transform_tables(sources)
    small = pl.pallas_call(
        transform_kernel,
        in_specs=[vmem] * 3 + [hbm] * 5,
        out_specs=[vmem] * CHUNKS,
        out_shape=[jax.ShapeDtypeStruct((COLUMNS, KEPT // CHUNKS), BF16)] * CHUNKS,
        scratch_shapes=[pltpu.VMEM(t.shape, t.dtype) for t in tables]
        + [
            pltpu.VMEM((BASE * COLUMNS, BASE), F32),
            pltpu.VMEM((64 * COLUMNS, BASE), F32),
            pltpu.SemaphoreType.DMA((len(tables),)),
        ],
        compiler_params=pltpu.CompilerParams(vmem_limit_bytes=32 * 1024 * 1024),
        name="transform",
    )(received, cosine, sine, *map(jnp.asarray, tables))

    mine, theirs = ring_gather(small, parts)
    back = order.T
    first, kv = gather_attend(core_here, guest, back, mine + theirs)
    returned = lax.ppermute(first, "yhi", SWAP)
    kept = attend(core_here, own, back, kv)
    return jnp.where(
        head == 0, jnp.stack([kept, returned]), jnp.stack([returned, kept])
    )


def solution(mesh):
    shape = mesh.devices.shape
    fine = Mesh(
        mesh.devices.reshape(shape[0], shape[1], 2, shape[2] // 4, 2),
        ("user", "heads", "yhi", "z", "core"),
    )
    tokens = ("user", "yhi", "z", "core")
    return jax.shard_map(
        on_device,
        mesh=fine,
        in_specs=(P(tokens, "heads"), P(tokens, "heads"), P("heads", tokens, None), P(tokens)),
        out_specs=P("heads", tokens, None),
        check_vma=False,
    )
```
